256 devices in a mesh: scene: 4 (over x), tile: 64 (over y, z, core).
Axes of the slice: x: 4, y: 4, z: 8, core: 2. Of those that a mesh axis runs over, the one named last changes fastest.
Arguments:
- blocks: bfloat16 [4, 128, 128, 512], P('scene', 'tile'), may hold values from -6 to 6
- block_position: int32 [4, 128], P('scene', 'tile'), may hold values from 0 to 15, as said below
- block_frame: int32 [4, 128], P('scene', 'tile'), may hold values from 0 to 7
- block_count: int32 [4, 64], P('scene', 'tile'), may hold values from 1 to 2, as said below
- weights: bfloat16 [8, 512, 512], replicated, may hold values from -0.25 to 0.25
- cotangent: bfloat16 [4, 16, 8, 128, 512], P('scene', None, None, 'tile'), may hold values from -6 to 6
Outputs:
- mixed: bfloat16 [4, 16, 8, 128, 512], P('scene', None, None, 'tile')
- input_grad: bfloat16 [4, 128, 128, 512], P('scene', 'tile')
- weight_grad: float32 [2, 2048, 512], P(None, ('scene', 'tile'))
The draws below stay inside these ranges and needn't reach their ends.
Inputs may be any that keep to these rules, and one draw needn't show every extreme that they name: `block_position`: together with block_frame, each of the 128 pairs of position and frame of a scene is named by exactly one slot of that scene. `block_count`: slots at or past a device's count are ignored; some device of each scene uses all 2.
All inputs are finite; a program needn't handle non-finite values.
Results may differ from the reference program's by a relative error of at most 0.019.
Values may be sent and summed in bfloat16 or wider, within the bound.
A program may use at most 64 MiB of HBM per device.

```python
from functools import partial
import jax
import jax.numpy as jnp
from jax import lax

D = 512
HEADS = 16
HEAD_DIM = 32
CELLS = 128
FRAMES = 8
SLOT_DEV = 2
SCENES = 4
BLOCKS = 128
POSITIONS = 16
N_TILE = 64


def scene_layout(scene_key):
    order = jax.random.permutation(jax.random.fold_in(scene_key, 1), BLOCKS).astype(jnp.int32)
    positions = order // FRAMES
    frame_ids = order % FRAMES
    counts = jax.random.randint(jax.random.fold_in(scene_key, 4), (N_TILE,), 1, SLOT_DEV + 1)
    chosen = jax.random.randint(jax.random.fold_in(scene_key, 5), (), 0, N_TILE)
    counts = counts.at[chosen].set(SLOT_DEV)
    return (positions.astype(jnp.int32), frame_ids.astype(jnp.int32), counts.astype(jnp.int32))


def shared_layout(key):
    scene_keys = jax.random.split(key, SCENES)
    return jax.vmap(scene_layout)(scene_keys)


def draw_block_position(key, part):
    return shared_layout(key)[0]


def draw_block_frame(key, part):
    return shared_layout(key)[1]


def draw_block_count(key, part):
    return shared_layout(key)[2]


def block_scale(own_key, shape, pieces, low, largest):
    factor_of, own = 1.0, jax.random.fold_in(own_key, 6)
    for position, blocks in pieces:
        heights = jnp.exp(jax.random.uniform(jax.random.fold_in(own, position), (blocks,), jnp.float32, low / len(pieces), largest / len(pieces)))
        factor_of = factor_of * jnp.repeat(heights, shape[position] // blocks).reshape([-1 if axis == position else 1 for axis in range(len(shape))])
    return factor_of


def bell_draw(stream_key, extent, deviation, most, shards=(), held_as=jnp.bfloat16):
    array = jax.random.normal(stream_key, extent, jnp.float32) * deviation
    if len(shards) > 0:
        array = block_scale(stream_key, extent, shards, -0.22, 0.18) * array
    return jnp.clip(array, min=-most, max=most).astype(held_as)


def setup_inputs(seed: int = 0) -> dict:
    key_of = jax.random.split(jax.random.key(seed), 7)
    blocks = bell_draw(key_of[0], (SCENES, BLOCKS, CELLS, D), 1.0, 6.0, ((0, 4), (1, 64)))
    block_position = draw_block_position(jax.random.fold_in(key_of[6], 71), 0)
    block_frame = draw_block_frame(jax.random.fold_in(key_of[6], 71), 0)
    block_count = draw_block_count(jax.random.fold_in(key_of[6], 71), 0)
    weights = bell_draw(key_of[4], (8, D, D), D ** -0.5, 0.25)
    cotangent = bell_draw(key_of[5], (SCENES, POSITIONS, FRAMES, CELLS, D), 1.0, 6.0, ((0, 4), (3, 64)))
    return dict(blocks=blocks, block_position=block_position, block_frame=block_frame, block_count=block_count, weights=weights, cotangent=cotangent)


EPSILON = 1e-06

def norm_rows(values):
    return values * lax.rsqrt(lax.optimization_barrier(jnp.mean(values * values, axis=-1, keepdims=True)) + EPSILON)

def right_dot(left_rows, weight):
    return jnp.dot(left_rows, weight, preferred_element_type=jnp.float32)

def right_dot_t(grad_rows, weight):
    return lax.dot_general(grad_rows, weight, (((grad_rows.ndim - 1,), (1,)), ((), ())), preferred_element_type=jnp.float32)

def outer_sum(left_rows, grad_rows):
    left_flat = left_rows.reshape(-1, left_rows.shape[-1])
    grad_flat = grad_rows.reshape(-1, grad_rows.shape[-1])
    return lax.dot_general(left_flat, grad_flat, (((0,), (0,)), ((), ())), preferred_element_type=jnp.float32)

def split_heads(values):
    return values.reshape(values.shape[:-1] + (HEADS, HEAD_DIM))

def block_core(queries, key_rows, values):
    scores = jnp.einsum('bqhe,bkhe->bhqk', split_heads(queries), split_heads(key_rows), preferred_element_type=jnp.float32) * HEAD_DIM ** (-0.5)
    soft_weights = jax.nn.softmax(scores, axis=-1).astype(jnp.bfloat16)
    context = jnp.einsum('bhqk,bkhe->bqhe', soft_weights, split_heads(values), preferred_element_type=jnp.float32)
    return context.astype(jnp.bfloat16).reshape(queries.shape)

def frame_core(queries, key_rows, values, active):
    frame_index = jnp.arange(queries.shape[0])
    allowed = (frame_index[:, None] >= frame_index[None, :]) & active[None, :]
    scores = jnp.einsum('fche,gche->chfg', split_heads(queries), split_heads(key_rows), preferred_element_type=jnp.float32) * HEAD_DIM ** (-0.5)
    scores = jnp.where(allowed, scores, -1e+30)
    soft_weights = jax.nn.softmax(scores, axis=-1).astype(jnp.bfloat16)
    context = jnp.einsum('chfg,gche->fche', soft_weights, split_heads(values), preferred_element_type=jnp.float32)
    return context.astype(jnp.bfloat16).reshape(queries.shape)

def piece_forward(inputs, weight_set, core):
    normed = norm_rows(inputs.astype(jnp.float32)).astype(jnp.bfloat16)
    queries = right_dot(normed, weight_set[0]).astype(jnp.bfloat16)
    key_rows = right_dot(normed, weight_set[1]).astype(jnp.bfloat16)
    values = right_dot(normed, weight_set[2]).astype(jnp.bfloat16)
    context, core_back = jax.vjp(core, queries, key_rows, values)
    output = inputs.astype(jnp.float32) + right_dot(context, weight_set[3])
    return (output, (normed, context, core_back))

def piece_backward(inputs, weight_set, saved_parts, grad_out):
    normed, context, core_back = saved_parts
    grad_proj = outer_sum(context, grad_out)
    grad_context = right_dot_t(grad_out, weight_set[3]).astype(jnp.bfloat16)
    grad_query, grad_key, grad_value = core_back(grad_context)
    weight_grads = jnp.stack([outer_sum(normed, grad_query), outer_sum(normed, grad_key), outer_sum(normed, grad_value), grad_proj])
    grad_normed = right_dot_t(grad_query, weight_set[0]) + right_dot_t(grad_key, weight_set[1]) + right_dot_t(grad_value, weight_set[2])
    unused, norm_back = jax.vjp(norm_rows, inputs.astype(jnp.float32))
    grad_input = grad_out.astype(jnp.float32) + norm_back(grad_normed)[0]
    return (grad_input, weight_grads)

def reference(blocks, block_position, block_frame, block_count, weights, cotangent):
    spatial_w = weights[0:4]
    temporal_w = weights[4:8]
    slot_count = BLOCKS // N_TILE

    def spatial_forward(group_rows):
        output, unused = piece_forward(group_rows, spatial_w, block_core)
        return output.astype(jnp.bfloat16)

    def scene_step(grad_total, scene_inputs):
        scene_blocks, positions, frame_ids, counts, scene_cot = scene_inputs
        usable = jnp.arange(BLOCKS) % slot_count < jnp.repeat(counts, slot_count)
        groups = scene_blocks.reshape(N_TILE, slot_count, CELLS, D)
        states = lax.map(spatial_forward, groups).reshape(BLOCKS, CELLS, D)
        kept = jnp.where(usable[:, None, None], states.astype(jnp.float32), 0.0)
        grid = jnp.zeros((POSITIONS, FRAMES, CELLS, D), jnp.float32).at[positions, frame_ids].add(kept).astype(jnp.bfloat16)
        active = jnp.zeros((POSITIONS, FRAMES), jnp.float32).at[positions, frame_ids].add(usable.astype(jnp.float32)) > 0.5

        def temporal_step(running, position_inputs):
            state_rows, active_row, cot_rows = position_inputs
            output, saved_parts = piece_forward(state_rows, temporal_w, partial(frame_core, active=active_row))
            keep_mask = active_row[:, None, None]
            mixed_out = jnp.where(keep_mask, output, 0.0).astype(jnp.bfloat16)
            grad_out = jnp.where(keep_mask, cot_rows, jnp.zeros_like(cot_rows))
            state_grad, weight_grads = piece_backward(state_rows, temporal_w, saved_parts, grad_out)
            return (running + weight_grads, (mixed_out, state_grad.astype(jnp.bfloat16)))
        temporal_grads, (mixed_all, grid_grad) = lax.scan(temporal_step, jnp.zeros((4, D, D), jnp.float32), (grid, active, scene_cot))
        block_grad = jnp.where(usable[:, None, None], grid_grad[positions, frame_ids], jnp.zeros((), jnp.bfloat16))

        def spatial_step(running, group_inputs):
            group_rows, group_grad = group_inputs
            output, saved_parts = piece_forward(group_rows, spatial_w, block_core)
            grad_input, weight_grads = piece_backward(group_rows, spatial_w, saved_parts, group_grad)
            return (running + weight_grads, grad_input.astype(jnp.bfloat16))
        spatial_grads, input_grads = lax.scan(spatial_step, jnp.zeros((4, D, D), jnp.float32), (groups, block_grad.reshape(N_TILE, slot_count, CELLS, D)))
        grad_total = grad_total + jnp.stack([spatial_grads, temporal_grads])
        return (grad_total, (mixed_all, input_grads.reshape(BLOCKS, CELLS, D)))
    grad_total, (mixed, input_grad) = lax.scan(scene_step, jnp.zeros((2, 4, D, D), jnp.float32), (blocks, block_position, block_frame, block_count, cotangent))
    scaling = (SCENES * BLOCKS * CELLS) ** (-0.5)
    return (mixed, input_grad, grad_total.reshape(2, 4 * D, D) * scaling)
```

```python
import jax
import jax.numpy as jnp
from jax import lax
from jax.experimental import pallas as pl
from jax.experimental.pallas import tpu as pltpu
from jax.sharding import PartitionSpec as P

MESH = pl.DeviceIdType.MESH
N_X, N_Y, N_Z = 4, 4, 8


def tile_index(y, z, core):
    return (y * N_Z + z) * 2 + core


def exchange(recv, send_sem, recv_sem, peers):
    for slot, (source, peer) in enumerate(peers):
        pltpu.make_async_remote_copy(
            src_ref=source,
            dst_ref=recv.at[slot],
            send_sem=send_sem,
            recv_sem=recv_sem,
            device_id=peer,
            device_id_type=MESH,
        ).start()
    pltpu.make_async_copy(recv, recv, send_sem).wait()
    pltpu.make_async_copy(recv, recv, recv_sem).wait()


def scatter_kernel(parts, out, sum_c, sum_x, sum_y, got_c, got_x, got_y, got_z, send_sem, recv_sem):
    x = lax.axis_index("scene")
    t = lax.axis_index("tile")
    core, z, y = lax.rem(t, 2), lax.rem(t // 2, N_Z), t // (2 * N_Z)
    peers_c = [(x, tile_index(y, z, 1 - core))]
    peers_x = [(lax.rem(x + d, N_X), t) for d in range(1, N_X)]
    peers_y = [(x, tile_index(lax.rem(y + d, N_Y), z, core)) for d in range(1, N_Y)]
    peers_z = [(x, tile_index(y, lax.rem(z + d, N_Z), core)) for d in range(1, N_Z)]
    barrier = pltpu.get_barrier_semaphore()
    for peer in peers_c + peers_x + peers_y + peers_z:
        pl.semaphore_signal(barrier, inc=1, device_id=peer, device_id_type=MESH)
    pl.semaphore_wait(barrier, 1 + N_X - 1 + N_Y - 1 + N_Z - 1)
    f32 = jnp.float32
    exchange(got_c, send_sem.at[0], recv_sem.at[0], [(parts.at[1 - core], peers_c[0])])

    @pl.loop(0, N_X)
    def _(i):
        for j in range(N_Y):
            sum_c[i, j] = (parts[core, i, j].astype(f32) + got_c[0, i, j].astype(f32)).astype(jnp.bfloat16)

    exchange(
        got_x,
        send_sem.at[1],
        recv_sem.at[1],
        [(sum_c.at[lax.rem(x + d, N_X)], peers_x[d - 1]) for d in range(1, N_X)],
    )
    for j in range(N_Y):
        total = sum_c[x, j].astype(f32)
        for d in range(N_X - 1):
            total += got_x[d, j].astype(f32)
        sum_x[j] = total.astype(jnp.bfloat16)
    exchange(
        got_y,
        send_sem.at[2],
        recv_sem.at[2],
        [(sum_x.at[lax.rem(y + d, N_Y)], peers_y[d - 1]) for d in range(1, N_Y)],
    )
    total = sum_x[y].astype(f32)
    for d in range(N_Y - 1):
        total += got_y[d].astype(f32)
    sum_y[...] = total.astype(jnp.bfloat16)
    exchange(
        got_z,
        send_sem.at[3],
        recv_sem.at[3],
        [(sum_y.at[lax.rem(z + d, N_Z)], peers_z[d - 1]) for d in range(1, N_Z)],
    )
    total = sum_y[z].astype(f32)
    for d in range(N_Z - 1):
        total += got_z[d].astype(f32)
    out[...] = total


def scatter_sum(stacked):
    pieces, rows, width = stacked.shape
    unit = (32, 256)
    parts = stacked.reshape(2, N_X, N_Y, N_Z, 2, 8, 2, 256).transpose(4, 1, 2, 3, 0, 6, 5, 7)
    parts = parts.reshape((2, N_X, N_Y, N_Z) + unit).astype(jnp.bfloat16)
    bf16 = jnp.bfloat16
    out = pl.pallas_call(
        scatter_kernel,
        out_shape=jax.ShapeDtypeStruct(unit, jnp.float32),
        in_specs=[pl.BlockSpec(memory_space=pltpu.VMEM)],
        out_specs=pl.BlockSpec(memory_space=pltpu.VMEM),
        scratch_shapes=[
            pltpu.VMEM((N_X, N_Y, N_Z) + unit, bf16),
            pltpu.VMEM((N_Y, N_Z) + unit, bf16),
            pltpu.VMEM((N_Z,) + unit, bf16),
            pltpu.VMEM((1, N_X, N_Y, N_Z) + unit, bf16),
            pltpu.VMEM((N_X - 1, N_Y, N_Z) + unit, bf16),
            pltpu.VMEM((N_Y - 1, N_Z) + unit, bf16),
            pltpu.VMEM((N_Z - 1,) + unit, bf16),
            pltpu.SemaphoreType.DMA((4,)),
            pltpu.SemaphoreType.DMA((4,)),
        ],
        compiler_params=pltpu.CompilerParams(
            collective_id=0, has_side_effects=True, vmem_limit_bytes=40 * 1024 * 1024
        ),
    )(parts)
    return out.reshape(2, 2, 8, 256).transpose(0, 2, 1, 3).reshape(2, 8, 512)

HEADS = 16
HEAD_DIM = 32


EPSILON = 1e-06


def norm_rows(values):
    return values * lax.rsqrt(jnp.mean(values * values, axis=-1, keepdims=True) + EPSILON)


def right_dot(left_rows, weight):
    return jnp.dot(left_rows, weight, preferred_element_type=jnp.float32)


def right_dot_t(grad_rows, weight):
    return lax.dot_general(
        grad_rows,
        weight,
        (((grad_rows.ndim - 1,), (1,)), ((), ())),
        preferred_element_type=jnp.float32,
    )


def outer_sum(left_rows, grad_rows):
    left_flat = left_rows.reshape(-1, left_rows.shape[-1])
    grad_flat = grad_rows.reshape(-1, grad_rows.shape[-1])
    return lax.dot_general(
        left_flat, grad_flat, (((0,), (0,)), ((), ())), preferred_element_type=jnp.float32
    )


def split_heads(values):
    return values.reshape(values.shape[:-1] + (HEADS, HEAD_DIM))


def block_core(queries, key_rows, values):
    scores = jnp.einsum(
        "bqhe,bkhe->bhqk",
        split_heads(queries),
        split_heads(key_rows),
        preferred_element_type=jnp.float32,
    ) * HEAD_DIM ** (-0.5)
    soft_weights = jax.nn.softmax(scores, axis=-1).astype(jnp.bfloat16)
    context = jnp.einsum(
        "bhqk,bkhe->bqhe", soft_weights, split_heads(values), preferred_element_type=jnp.float32
    )
    return context.astype(jnp.bfloat16).reshape(queries.shape)


def frame_core(queries, key_rows, values, active):
    frame_index = jnp.arange(queries.shape[0])
    allowed = (frame_index[:, None] >= frame_index[None, :]) & active[None, :]
    scores = jnp.einsum(
        "fche,gche->chfg",
        split_heads(queries),
        split_heads(key_rows),
        preferred_element_type=jnp.float32,
    ) * HEAD_DIM ** (-0.5)
    scores = jnp.where(allowed, scores, -1e30)
    soft_weights = jax.nn.softmax(scores, axis=-1).astype(jnp.bfloat16)
    context = jnp.einsum(
        "chfg,gche->fche", soft_weights, split_heads(values), preferred_element_type=jnp.float32
    )
    return context.astype(jnp.bfloat16).reshape(queries.shape)


def piece_forward(inputs, weight_set, core):
    normed = norm_rows(inputs.astype(jnp.float32)).astype(jnp.bfloat16)
    queries = right_dot(normed, weight_set[0]).astype(jnp.bfloat16)
    key_rows = right_dot(normed, weight_set[1]).astype(jnp.bfloat16)
    values = right_dot(normed, weight_set[2]).astype(jnp.bfloat16)
    context, core_back = jax.vjp(core, queries, key_rows, values)
    output = inputs.astype(jnp.float32) + right_dot(context, weight_set[3])
    return (output, (normed, context, core_back))


def piece_backward(inputs, weight_set, saved_parts, grad_out):
    normed, context, core_back = saved_parts
    grad_proj = outer_sum(context, grad_out)
    grad_context = right_dot_t(grad_out, weight_set[3]).astype(jnp.bfloat16)
    grad_query, grad_key, grad_value = core_back(grad_context)
    weight_grads = jnp.stack(
        [
            outer_sum(normed, grad_query),
            outer_sum(normed, grad_key),
            outer_sum(normed, grad_value),
            grad_proj,
        ]
    )
    grad_normed = (
        right_dot_t(grad_query, weight_set[0])
        + right_dot_t(grad_key, weight_set[1])
        + right_dot_t(grad_value, weight_set[2])
    )
    unused, norm_back = jax.vjp(norm_rows, inputs.astype(jnp.float32))
    grad_input = grad_out.astype(jnp.float32) + norm_back(grad_normed)[0]
    return (grad_input, weight_grads)


def place_stack(placing, rows):
    return jnp.einsum("ms,kse->kme", placing, rows, preferred_element_type=jnp.float32).astype(
        jnp.bfloat16
    )


def unplace_stack(placing, rows):
    return jnp.einsum("ms,kme->kse", placing, rows, preferred_element_type=jnp.float32).astype(
        jnp.bfloat16
    )


def body(blocks, block_position, block_frame, block_count, weights, cotangent):
    tile_count = lax.axis_size("tile")
    own_blocks = blocks[0]
    slot_count = own_blocks.shape[0]
    cell_count = own_blocks.shape[1]
    model_width = own_blocks.shape[2]
    position_count = cotangent.shape[1]
    frame_count = cotangent.shape[2]
    cell_share = cotangent.shape[3]
    spatial_w = weights[0:4]
    temporal_w = weights[4:8]
    usable = jnp.arange(slot_count) < block_count[0, 0]
    slot_tag = jnp.where(usable, block_position[0] * frame_count + block_frame[0], -1)
    source_out, spatial_saved = piece_forward(own_blocks, spatial_w, block_core)
    states = source_out.astype(jnp.bfloat16)
    grid_shape = (position_count, frame_count, cell_share, model_width)
    entry_ids = jnp.arange(position_count * frame_count)
    cot_rows = cotangent[0]
    outgoing = states.reshape(slot_count, tile_count, cell_share, model_width)
    tag_rows = jnp.broadcast_to(slot_tag[:, None], (slot_count, tile_count))
    received, tags_in = (
        lax.all_to_all(outgoing, "tile", split_axis=1, concat_axis=1, tiled=True),
        lax.all_to_all(tag_rows, "tile", split_axis=1, concat_axis=1, tiled=True),
    )
    placing_mask = tags_in.reshape(-1)[None, :] == entry_ids[:, None]
    placing = placing_mask.astype(jnp.bfloat16)
    active = jnp.any(placing_mask, axis=1).reshape(position_count, frame_count)
    grid = place_stack(
        placing, received.reshape(1, slot_count * tile_count, cell_share * model_width)
    )[0].reshape(grid_shape)

    def grid_core(queries, key_rows, values):
        return jax.vmap(frame_core)(queries, key_rows, values, active)

    temporal_out, temporal_saved = piece_forward(grid, temporal_w, grid_core)
    keep_mask = active[:, :, None, None]
    mixed_out = jnp.where(keep_mask, temporal_out, 0.0).astype(jnp.bfloat16)
    grad_out = jnp.where(keep_mask, cot_rows, jnp.zeros_like(cot_rows))
    grid_grad32, temporal_grads = piece_backward(grid, temporal_w, temporal_saved, grad_out)
    back_grid = grid_grad32.astype(jnp.bfloat16).reshape(
        1, position_count * frame_count, cell_share * model_width
    )
    sendback = unplace_stack(placing, back_grid)[0].reshape(
        slot_count, tile_count, cell_share, model_width
    )
    returned = lax.all_to_all(sendback, "tile", split_axis=1, concat_axis=1, tiled=True)
    block_grad = returned.reshape(slot_count, cell_count, model_width)
    scaling = (lax.axis_size("scene") * tile_count * slot_count * cell_count) ** (-0.5)
    input_grad32, spatial_grads = piece_backward(own_blocks, spatial_w, spatial_saved, block_grad)
    input_grad = input_grad32.astype(jnp.bfloat16)
    stacked = jnp.stack(
        [
            spatial_grads.reshape(4 * model_width, model_width),
            temporal_grads.reshape(4 * model_width, model_width),
        ]
    )
    grad_total = scatter_sum(stacked)
    return (mixed_out[None], input_grad[None], grad_total * scaling)


def solution(mesh):
    return jax.shard_map(
        body,
        mesh=mesh,
        in_specs=(
            P("scene", "tile", None, None),
            P("scene", "tile"),
            P("scene", "tile"),
            P("scene", "tile"),
            P(),
            P("scene", None, None, "tile", None),
        ),
        out_specs=(
            P("scene", None, None, "tile", None),
            P("scene", "tile", None, None),
            P(None, ("scene", "tile"), None),
        ),
        check_vma=False,
    )
```

```python
import functools

import jax
import jax.numpy as jnp
from jax import lax
from jax.experimental import pallas as pl
from jax.experimental.pallas import tpu as pltpu
from jax.sharding import PartitionSpec as P

MESH = pl.DeviceIdType.MESH
N_X, N_Y, N_Z, N_TILE = 4, 4, 8, 64
HEADS, HEAD_DIM = 16, 32
WIDTH, ROWS, HALF = 512, 256, 128
FRAMES = 8
GROUP = 4
EPSILON = 1e-06
SPATIAL, TEMPORAL = 0, 1
BF16, F32 = jnp.bfloat16, jnp.float32
EXP2_SCALE = HEAD_DIM ** (-0.5) * 1.4426950408889634
SCALE = HEAD_DIM ** (-0.5)
TAGS, STATES, GRADS, LAST, CORE, FIRST_X, FIRST_Y, SECOND_Y, SECOND_X = 0, 1, 2, 3, 4, 12, 14, 16, 18
N_SEM = 20


def dot(left, right):
    return jnp.dot(left, right, preferred_element_type=F32)


def dot_tn(left, right):
    return lax.dot_general(left, right, (((0,), (0,)), ((), ())), preferred_element_type=F32)


def dot_nt(left, right):
    return lax.dot_general(left, right, (((1,), (1,)), ((), ())), preferred_element_type=F32)


def iota(shape, axis):
    return lax.broadcasted_iota(jnp.int32, shape, axis)


def tile_index(y, z, core):
    return (y * N_Z + z) * 2 + core


def inverse_norm(rows):
    return lax.rsqrt(jnp.mean(rows * rows, axis=-1, keepdims=True) + EPSILON)


def kernel(
    position,
    frame,
    count,
    blocks,
    weights,
    cot,
    mixed_out,
    grad_out,
    weight_out,
    mask,
    tag_out,
    tag_in,
    spread,
    box_out,
    box_in,
    normed_t,
    query_t,
    key_t,
    value_t,
    key_n,
    value_n,
    context_t,
    soft_t,
    grad_context_t,
    grad_t,
    grid,
    parts,
    got_core,
    sum_a,
    sum_b,
    got_a,
    got_b,
    sum_a2,
    sum_b2,
    got_a2,
    got_b2,
    last,
    got_last,
    send_sem,
    recv_sem,
):
    x = lax.axis_index("scene")
    t = lax.axis_index("tile")
    core, z, y = lax.rem(t, 2), lax.rem(t // 2, N_Z), t // (2 * N_Z)
    peer_core = (x, tile_index(y, z, 1 - core))
    peers_x = [(lax.rem(x + d, N_X), t) for d in range(1, N_X)]
    peers_y = [(x, tile_index(lax.rem(y + d, N_Y), z, core)) for d in range(1, N_Y)]
    peers_z = [(x, tile_index(y, lax.rem(z + d, N_Z), core)) for d in range(1, N_Z)]

    barrier = pltpu.get_barrier_semaphore()

    @pl.loop(1, N_TILE)
    def _(d):
        pl.semaphore_signal(
            barrier, inc=1, device_id=(x, lax.rem(t + d, N_TILE)), device_id_type=MESH
        )

    for peer in peers_x:
        pl.semaphore_signal(barrier, inc=1, device_id=peer, device_id_type=MESH)

    def start(source, target, sem, peer):
        pltpu.make_async_remote_copy(
            src_ref=source,
            dst_ref=target,
            send_sem=send_sem.at[sem],
            recv_sem=recv_sem.at[sem],
            device_id=peer,
            device_id_type=MESH,
        ).start()

    def wait(sems, ref, sem):
        pltpu.make_async_copy(ref, ref, sems.at[sem]).wait()

    def send_all(outgoing, incoming, sem):
        @pl.loop(1, N_TILE)
        def _(d):
            to = lax.rem(t + d, N_TILE)
            start(outgoing(to), incoming.at[t], sem, (x, to))

    def project(piece, rows):
        scaled = (rows * inverse_norm(rows)).astype(BF16)
        normed_t[piece] = scaled.T
        first = 4 * piece
        query_t[piece] = dot(scaled, weights[first]).astype(BF16).T
        keys = dot(scaled, weights[first + 1]).astype(BF16)
        key_n[piece] = keys
        key_t[piece] = keys.T
        values = dot(scaled, weights[first + 2]).astype(BF16)
        value_n[piece] = values
        value_t[piece] = values.T

    def one_head(group_t, h):
        owner = iota((HALF, HALF), 0) // HEAD_DIM
        return jnp.where(owner == h, group_t, jnp.zeros_like(group_t))

    def attend(piece):
        @pl.loop(0, HEADS // GROUP)
        def _(g):
            feats = pl.ds(pl.multiple_of(g * HALF, HALF), HALF)
            for b in range(2):
                own = slice(b * HALF, (b + 1) * HALF)
                queries = query_t[piece, feats, own]
                keys = key_n[piece, own, feats]
                for h in range(GROUP):
                    scores = dot(keys, one_head(queries, h))
                    if piece == TEMPORAL:
                        scores = jnp.where(mask[...] > 0.5, scores, -1e30)
                    top = jnp.max(scores, axis=0, keepdims=True)
                    powers = jnp.exp2((scores - top) * EXP2_SCALE)
                    share = 1.0 / jnp.sum(powers, axis=0, keepdims=True)
                    soft = (powers * share).astype(BF16)
                    soft_t[piece, g, b, h] = soft
                    head = pl.ds(pl.multiple_of(g * HALF + h * HEAD_DIM, HEAD_DIM), HEAD_DIM)
                    context_t[piece, head, own] = dot(value_t[piece, head, own], soft).astype(BF16)

    def attend_back(piece):
        @pl.loop(0, HEADS // GROUP)
        def _(g):
            feats = pl.ds(pl.multiple_of(g * HALF, HALF), HALF)
            for b in range(2):
                own = slice(b * HALF, (b + 1) * HALF)
                grads = grad_context_t[piece, feats, own]
                values = value_n[piece, own, feats]
                for h in range(GROUP):
                    head = pl.ds(pl.multiple_of(g * HALF + h * HEAD_DIM, HEAD_DIM), HEAD_DIM)
                    soft = soft_t[piece, g, b, h]
                    wide = soft.astype(F32)
                    grad_soft = dot(values, one_head(grads, h))
                    mean = jnp.sum(wide * grad_soft, axis=0, keepdims=True)
                    grad_scores = (wide * (grad_soft - mean) * SCALE).astype(BF16)
                    grad_t[piece, 0, head, own] = dot(key_t[piece, head, own], grad_scores).astype(BF16)
                    grad_t[piece, 1, head, own] = dot_nt(query_t[piece, head, own], grad_scores).astype(BF16)
                    grad_t[piece, 2, head, own] = dot_nt(grad_context_t[piece, head, own], soft).astype(BF16)

    def input_back(piece, rows, rest):
        first = 4 * piece
        grad_normed_t = (
            dot(weights[first], grad_t[piece, 0])
            + dot(weights[first + 1], grad_t[piece, 1])
            + dot(weights[first + 2], grad_t[piece, 2])
        )
        grad_normed = grad_normed_t.T
        inverse = inverse_norm(rows)
        scaled = rows * inverse
        along = jnp.mean(scaled * grad_normed, axis=-1, keepdims=True)
        return rest.astype(F32) + inverse * (grad_normed - scaled * along)

    def put_part(piece, w, s, product):
        split = product.reshape(N_Y * N_Z, 2, 8, 2 * HALF)
        for c in range(2):
            unit = jnp.concatenate([split[:, c, :, :HALF], split[:, c, :, HALF:]], axis=1)
            parts[piece, c, w, s] = unit.astype(BF16).reshape(N_Y, N_Z, 16, HALF)

    def send_core(piece, w):
        start(parts.at[piece, 1 - core, w], got_core.at[piece, w], CORE + 4 * piece + w, peer_core)

    def context_sum(piece, rest):
        for s in range(2):
            put_part(piece, 3, s, dot(context_t[piece], rest[:, 2 * HALF * s : 2 * HALF * (s + 1)]))
        send_core(piece, 3)

    def normed_sums(piece):
        for w in range(3):
            for s in range(2):
                chunk = slice(2 * HALF * s, 2 * HALF * (s + 1))
                put_part(piece, w, s, dot_nt(normed_t[piece], grad_t[piece, w, chunk]))
            send_core(piece, w)

    def sum_core(piece):
        for w in range(4):
            wait(recv_sem, got_core.at[piece, w], CORE + 4 * piece + w)
            sum_a[piece, w] = (
                parts[piece, core, w, 0].astype(F32) + got_core[piece, w, 0].astype(F32)
            ).astype(BF16)
            for j in range(N_Y):
                sum_b[piece, j, w] = (
                    parts[piece, core, w, 1, j].astype(F32) + got_core[piece, w, 1, j].astype(F32)
                ).astype(BF16)
        for d in range(1, N_X):
            start(sum_a.at[piece, lax.rem(x + d, N_X)], got_a.at[piece, d - 1], FIRST_X + piece, peers_x[d - 1])
        for d in range(1, N_Y):
            start(sum_b.at[piece, lax.rem(y + d, N_Y)], got_b.at[piece, d - 1], FIRST_Y + piece, peers_y[d - 1])

    def add_up(own, got, n):
        total = own.astype(F32)
        for d in range(n - 1):
            total += got[d].astype(F32)
        return total

    def sum_first(piece):
        wait(recv_sem, got_a.at[piece], FIRST_X + piece)
        sum_a2[piece] = add_up(sum_a[piece, x], [got_a[piece, d] for d in range(N_X - 1)], N_X).astype(BF16)
        for d in range(1, N_Y):
            start(sum_a2.at[piece, lax.rem(y + d, N_Y)], got_a2.at[piece, d - 1], SECOND_Y + piece, peers_y[d - 1])
        wait(recv_sem, got_b.at[piece], FIRST_Y + piece)
        sum_b2[piece] = add_up(sum_b[piece, y], [got_b[piece, d] for d in range(N_Y - 1)], N_Y).astype(BF16)
        for d in range(1, N_X):
            start(sum_b2.at[piece, lax.rem(x + d, N_X)], got_b2.at[piece, d - 1], SECOND_X + piece, peers_x[d - 1])

    def sum_second(piece):
        wait(recv_sem, got_a2.at[piece], SECOND_Y + piece)
        last[:, piece, 0] = add_up(sum_a2[piece, y], [got_a2[piece, d] for d in range(N_Y - 1)], N_Y).astype(BF16)
        wait(recv_sem, got_b2.at[piece], SECOND_X + piece)
        last[:, piece, 1] = add_up(sum_b2[piece, x], [got_b2[piece, d] for d in range(N_X - 1)], N_X).astype(BF16)

    project(SPATIAL, blocks[...].astype(F32))

    lane = iota((1, HALF), 1)
    tags = [
        jnp.where(s < count[0, 0], position[0, s] * FRAMES + frame[0, s], -1) for s in range(2)
    ]
    tag_out[...] = jnp.where(lane < N_TILE, tags[0], tags[1])
    tag_in[t] = tag_out[...]
    pl.semaphore_wait(barrier, N_TILE - 1 + N_X - 1)
    send_all(lambda to: tag_out, tag_in, TAGS)

    attend(SPATIAL)
    states = blocks[...].astype(F32) + dot_tn(context_t[SPATIAL], weights[3])
    for s in range(2):
        for k in range(4):
            spread[pl.ds(4 * s + k, HALF, stride=8), :] = states[
                s * HALF : (s + 1) * HALF, k * HALF : (k + 1) * HALF
            ]
    box_out[0] = spread[...].astype(BF16).reshape(N_TILE, 16, HALF)
    box_in[0, t] = box_out[0, t]
    send_all(lambda to: box_out.at[0, to], box_in.at[0], STATES)

    wait(recv_sem, tag_in.at[pl.ds(0, N_TILE - 1)], TAGS)
    entry = iota((N_TILE, HALF), 1)
    placing = jnp.concatenate(
        [
            jnp.where(tag_in[:, 0, N_TILE * s : N_TILE * s + 1] == entry, 1.0, 0.0)
            for s in range(2)
        ],
        axis=0,
    ).astype(BF16)
    active = dot_tn(placing, jnp.ones((HALF, HALF), BF16))
    key_row, query_row = iota((HALF, HALF), 0), iota((HALF, HALF), 1)
    seen = (key_row // FRAMES == query_row // FRAMES) & (key_row <= query_row)
    mask[...] = jnp.where(seen, active, 0.0)
    active_wide = jnp.concatenate([active] * 4, axis=1) > 0.5
    natural = iota((ROWS, ROWS), 1)
    by_cell = iota((ROWS, ROWS), 0)
    order = jnp.where(
        natural == lax.rem(by_cell, HALF) * 2 + by_cell // HALF, 1.0, 0.0
    ).astype(BF16)
    cot_rows = dot(order, cot[...])
    rest = jnp.concatenate(
        [jnp.where(active_wide, cot_rows[j * HALF : (j + 1) * HALF], 0.0) for j in range(2)], axis=0
    ).astype(BF16)
    grad_context_t[TEMPORAL] = dot_nt(weights[7], rest).astype(BF16)

    wait(recv_sem, box_in.at[0, pl.ds(0, N_TILE - 1)], STATES)
    spread[...] = box_in[0].reshape(N_TILE * 16, HALF).astype(F32)
    for j in range(2):
        rows = jnp.concatenate(
            [
                jnp.concatenate(
                    [spread[pl.ds(8 * j + 4 * s + k, N_TILE, stride=16), :] for k in range(4)], axis=1
                )
                for s in range(2)
            ],
            axis=0,
        ).astype(BF16)
        grid[j * HALF : (j + 1) * HALF] = dot_tn(placing, rows)

    project(TEMPORAL, grid[...])
    attend(TEMPORAL)
    attend_back(TEMPORAL)
    grid_grad = input_back(TEMPORAL, grid[...], rest).astype(BF16)
    for j in range(2):
        back = dot(placing, grid_grad[j * HALF : (j + 1) * HALF])
        for s in range(2):
            for k in range(4):
                spread[pl.ds(8 * j + 4 * s + k, N_TILE, stride=16), :] = back[
                    s * N_TILE : (s + 1) * N_TILE, k * HALF : (k + 1) * HALF
                ]
    box_out[1] = spread[...].astype(BF16).reshape(N_TILE, 16, HALF)
    box_in[1, t] = box_out[1, t]
    send_all(lambda to: box_out.at[1, to], box_in.at[1], GRADS)

    context_sum(TEMPORAL, rest)
    normed_sums(TEMPORAL)
    temporal = grid[...] + dot_tn(context_t[TEMPORAL], weights[7])
    mixed = jnp.concatenate(
        [jnp.where(active_wide, temporal[j * HALF : (j + 1) * HALF], 0.0) for j in range(2)], axis=0
    ).astype(BF16)
    mixed_out[...] = dot_tn(order, mixed).astype(BF16)

    wait(recv_sem, box_in.at[1, pl.ds(0, N_TILE - 1)], GRADS)
    spread[...] = box_in[1].reshape(N_TILE * 16, HALF).astype(F32)
    rest = jnp.concatenate(
        [
            jnp.concatenate([spread[pl.ds(4 * s + k, HALF, stride=8), :] for k in range(4)], axis=1)
            for s in range(2)
        ],
        axis=0,
    ).astype(BF16)
    context_sum(SPATIAL, rest)
    grad_context_t[SPATIAL] = dot_nt(weights[3], rest).astype(BF16)
    sum_core(TEMPORAL)
    attend_back(SPATIAL)
    normed_sums(SPATIAL)
    sum_first(TEMPORAL)
    sum_core(SPATIAL)
    grad_out[...] = input_back(SPATIAL, blocks[...].astype(F32), rest).astype(BF16)
    sum_second(TEMPORAL)
    sum_first(SPATIAL)
    sum_second(SPATIAL)
    for d in range(1, N_Z):
        start(last.at[lax.rem(z + d, N_Z)], got_last.at[d - 1], LAST, peers_z[d - 1])
    wait(recv_sem, got_last, LAST)
    scaling = (N_X * N_TILE * ROWS) ** (-0.5)
    total = add_up(last[z], [got_last[d] for d in range(N_Z - 1)], N_Z) * scaling
    for piece in range(2):
        for s in range(2):
            for half in range(2):
                column = (2 * s + half) * HALF
                weight_out[piece, :, column : column + HALF] = total[piece, s, 8 * half : 8 * half + 8]

    wait(send_sem, tag_in.at[pl.ds(0, N_TILE - 1)], TAGS)
    wait(send_sem, box_in.at[0, pl.ds(0, N_TILE - 1)], STATES)
    wait(send_sem, box_in.at[1, pl.ds(0, N_TILE - 1)], GRADS)
    wait(send_sem, got_last, LAST)
    for piece in range(2):
        for w in range(4):
            wait(send_sem, got_core.at[piece, w], CORE + 4 * piece + w)
        wait(send_sem, got_a.at[piece], FIRST_X + piece)
        wait(send_sem, got_b.at[piece], FIRST_Y + piece)
        wait(send_sem, got_a2.at[piece], SECOND_Y + piece)
        wait(send_sem, got_b2.at[piece], SECOND_X + piece)


def body(blocks, block_position, block_frame, block_count, weights, cotangent):
    unit = (16, HALF)
    pair = (2, ROWS, WIDTH)
    turned = (2, WIDTH, ROWS)
    vmem = pl.BlockSpec(memory_space=pltpu.VMEM)
    smem = pl.BlockSpec(memory_space=pltpu.SMEM)
    mixed, input_grad, weight_grad = pl.pallas_call(
        kernel,
        out_shape=(
            jax.ShapeDtypeStruct((ROWS, WIDTH), BF16),
            jax.ShapeDtypeStruct((ROWS, WIDTH), BF16),
            jax.ShapeDtypeStruct((2, 8, WIDTH), F32),
        ),
        in_specs=[smem, smem, smem, vmem, vmem, vmem],
        out_specs=(vmem, vmem, vmem),
        scratch_shapes=[
            pltpu.VMEM((HALF, HALF), F32),
            pltpu.VMEM((1, HALF), jnp.int32),
            pltpu.VMEM((N_TILE, 1, HALF), jnp.int32),
            pltpu.VMEM((N_TILE * 16, HALF), F32),
            pltpu.VMEM((2, N_TILE) + unit, BF16),
            pltpu.VMEM((2, N_TILE) + unit, BF16),
            pltpu.VMEM(turned, BF16),
            pltpu.VMEM(turned, BF16),
            pltpu.VMEM(turned, BF16),
            pltpu.VMEM(turned, BF16),
            pltpu.VMEM(pair, BF16),
            pltpu.VMEM(pair, BF16),
            pltpu.VMEM(turned, BF16),
            pltpu.VMEM((2, HEADS // GROUP, 2, GROUP, HALF, HALF), BF16),
            pltpu.VMEM(turned, BF16),
            pltpu.VMEM((2, 3, WIDTH, ROWS), BF16),
            pltpu.VMEM((ROWS, WIDTH), F32),
            pltpu.VMEM((2, 2, 4, 2, N_Y, N_Z) + unit, BF16),
            pltpu.VMEM((2, 4, 2, N_Y, N_Z) + unit, BF16),
            pltpu.VMEM((2, N_X, N_Y, N_Z) + unit, BF16),
            pltpu.VMEM((2, N_Y, N_X, N_Z) + unit, BF16),
            pltpu.VMEM((2, N_X - 1, N_Y, N_Z) + unit, BF16),
            pltpu.VMEM((2, N_Y - 1, N_X, N_Z) + unit, BF16),
            pltpu.VMEM((2, N_Y, N_Z) + unit, BF16),
            pltpu.VMEM((2, N_X, N_Z) + unit, BF16),
            pltpu.VMEM((2, N_Y - 1, N_Z) + unit, BF16),
            pltpu.VMEM((2, N_X - 1, N_Z) + unit, BF16),
            pltpu.VMEM((N_Z, 2, 2) + unit, BF16),
            pltpu.VMEM((N_Z - 1, 2, 2) + unit, BF16),
            pltpu.SemaphoreType.DMA((N_SEM,)),
            pltpu.SemaphoreType.DMA((N_SEM,)),
        ],
        compiler_params=pltpu.CompilerParams(
            collective_id=0, has_side_effects=True, vmem_limit_bytes=48 * 1024 * 1024
        ),
    )(
        block_position,
        block_frame,
        block_count,
        blocks.reshape(ROWS, WIDTH),
        weights,
        cotangent.reshape(ROWS, WIDTH),
    )
    return mixed.reshape(cotangent.shape), input_grad.reshape(blocks.shape), weight_grad


def solution(mesh):
    return jax.shard_map(
        body,
        mesh=mesh,
        in_specs=(
            P("scene", "tile", None, None),
            P("scene", "tile"),
            P("scene", "tile"),
            P("scene", "tile"),
            P(),
            P("scene", None, None, "tile", None),
        ),
        out_specs=(
            P("scene", None, None, "tile", None),
            P("scene", "tile", None, None),
            P(None, ("scene", "tile"), None),
        ),
        check_vma=False,
    )
```

```python
import functools

import jax
import jax.numpy as jnp
from jax import lax
from jax.experimental import pallas as pl
from jax.experimental.pallas import tpu as pltpu
from jax.sharding import PartitionSpec as P

MESH = pl.DeviceIdType.MESH
N_X, N_Y, N_Z, N_TILE = 4, 4, 8, 64
HEADS, HEAD_DIM = 16, 32
WIDTH, ROWS, HALF = 512, 256, 128
FRAMES = 8
GROUP = 4
EPSILON = 1e-06
SPATIAL, TEMPORAL = 0, 1
BF16, F32 = jnp.bfloat16, jnp.float32
EXP2_SCALE = HEAD_DIM ** (-0.5) * 1.4426950408889634
SCALE = HEAD_DIM ** (-0.5)
TAGS, STATES, GRADS, CORE, FIRST_X, FIRST_Y, SECOND_Y, SECOND_X, LAST = 0, 1, 2, 3, 11, 13, 15, 17, 19
N_SEM = 21


def dot(left, right):
    return jnp.dot(left, right, preferred_element_type=F32)


def dot_tn(left, right):
    return lax.dot_general(left, right, (((0,), (0,)), ((), ())), preferred_element_type=F32)


def dot_nt(left, right):
    return lax.dot_general(left, right, (((1,), (1,)), ((), ())), preferred_element_type=F32)


def iota(shape, axis):
    return lax.broadcasted_iota(jnp.int32, shape, axis)


def tile_index(y, z, core):
    return (y * N_Z + z) * 2 + core


def inverse_norm(rows):
    return lax.rsqrt(jnp.mean(rows * rows, axis=-1, keepdims=True) + EPSILON)


def kernel(
    position_in,
    frame_in,
    count_in,
    blocks_in,
    weights_in,
    cot_in,
    mixed_to,
    grad_to,
    weight_to,
    mixed_out,
    grad_out,
    weight_out,
    position,
    frame,
    count,
    blocks,
    weights,
    weights_t,
    cot,
    mask,
    tag_out,
    tag_in,
    spread,
    box_out,
    box_in,
    normed_n,
    normed_t,
    query_n,
    query_t,
    key_n,
    key_t,
    value_n,
    value_t,
    context_t,
    soft_t,
    grad_context_n,
    grad_context_t,
    grad_n,
    grid,
    parts,
    got_core,
    sum_a,
    sum_b,
    got_a,
    got_b,
    sum_a2,
    sum_b2,
    got_a2,
    got_b2,
    last,
    got_last,
    in_sem,
    out_sem,
    send_sem,
    recv_sem,
):
    loads = [
        pltpu.make_async_copy(source, target, in_sem.at[i])
        for i, (source, target) in enumerate(
            [
                (blocks_in, blocks),
                (weights_in.at[pl.ds(0, 3)], weights.at[pl.ds(0, 3)]),
                (position_in, position),
                (frame_in, frame),
                (count_in, count),
                (weights_in.at[pl.ds(3, 5)], weights.at[pl.ds(3, 5)]),
                (cot_in, cot),
            ]
        )
    ]
    for load in loads:
        load.start()
    stores = [
        pltpu.make_async_copy(source, target, out_sem.at[i])
        for i, (source, target) in enumerate(
            [(mixed_out, mixed_to), (grad_out, grad_to), (weight_out, weight_to)]
        )
    ]

    x = lax.axis_index("scene")
    t = lax.axis_index("tile")
    core, z, y = lax.rem(t, 2), lax.rem(t // 2, N_Z), t // (2 * N_Z)
    peer_core = (x, tile_index(y, z, 1 - core))
    peers_x = [(lax.rem(x + d, N_X), t) for d in range(1, N_X)]
    peers_y = [(x, tile_index(lax.rem(y + d, N_Y), z, core)) for d in range(1, N_Y)]
    peers_z = [(x, tile_index(y, lax.rem(z + d, N_Z), core)) for d in range(1, N_Z)]

    barrier = pltpu.get_barrier_semaphore()

    @pl.loop(1, N_TILE)
    def _(d):
        pl.semaphore_signal(
            barrier, inc=1, device_id=(x, lax.rem(t + d, N_TILE)), device_id_type=MESH
        )

    for peer in peers_x:
        pl.semaphore_signal(barrier, inc=1, device_id=peer, device_id_type=MESH)

    def start(source, target, sem, peer):
        pltpu.make_async_remote_copy(
            src_ref=source,
            dst_ref=target,
            send_sem=send_sem.at[sem],
            recv_sem=recv_sem.at[sem],
            device_id=peer,
            device_id_type=MESH,
        ).start()

    def wait(sems, ref, sem):
        pltpu.make_async_copy(ref, ref, sems.at[sem]).wait()

    def send_all(outgoing, incoming, sem):
        @pl.loop(1, N_TILE)
        def _(d):
            to = lax.rem(t + d, N_TILE)
            start(outgoing(to), incoming.at[t], sem, (x, to))

    def project(piece, rows):
        scaled = (rows * inverse_norm(rows)).astype(BF16)
        normed_n[piece] = scaled
        first = 4 * piece
        queries = dot(scaled, weights[first]).astype(BF16)
        query_n[piece] = queries
        query_t[...] = queries.T
        key_n[piece] = dot(scaled, weights[first + 1]).astype(BF16)
        values = dot(scaled, weights[first + 2]).astype(BF16)
        value_n[piece] = values
        value_t[...] = values.T

    def one_head(rows, h, axis):
        owner = iota((HALF, HALF), axis) // HEAD_DIM
        return jnp.where(owner == h, rows, jnp.zeros_like(rows))

    def by_head(rows, axis):
        return jnp.concatenate([one_head(rows, h, axis) for h in range(GROUP)], axis=1 - axis)

    def attend(piece):
        @pl.loop(0, HEADS // GROUP)
        def _(g):
            feats = pl.ds(pl.multiple_of(g * HALF, HALF), HALF)
            for b in range(2):
                own = slice(b * HALF, (b + 1) * HALF)
                queries = query_t[feats, own]
                keys = key_n[piece, own, feats]
                for h in range(GROUP):
                    scores = dot(keys, one_head(queries, h, 0))
                    if piece == TEMPORAL:
                        scores = jnp.where(mask[...] > 0.5, scores, -1e30)
                    top = jnp.max(scores, axis=0, keepdims=True)
                    powers = jnp.exp2((scores - top) * EXP2_SCALE)
                    share = 1.0 / jnp.sum(powers, axis=0, keepdims=True)
                    soft = (powers * share).astype(BF16)
                    soft_t[piece, g, b, :, h * HALF : (h + 1) * HALF] = soft
                    head = pl.ds(pl.multiple_of(g * HALF + h * HEAD_DIM, HEAD_DIM), HEAD_DIM)
                    context_t[piece, head, own] = dot(value_t[head, own], soft).astype(BF16)

    def attend_back(piece, lower, upper):
        @pl.loop(lower, upper)
        def _(g):
            feats = pl.ds(pl.multiple_of(g * HALF, HALF), HALF)
            for b in range(2):
                own = slice(b * HALF, (b + 1) * HALF)
                grads_t = grad_context_t[feats, own]
                values = value_n[piece, own, feats]
                soft = soft_t[piece, g, b]
                grad_scores, grad_queries = [], []
                for h in range(GROUP):
                    wide = soft[:, h * HALF : (h + 1) * HALF].astype(F32)
                    grad_soft = dot(values, one_head(grads_t, h, 0))
                    mean = jnp.sum(wide * grad_soft, axis=0, keepdims=True)
                    grad_scores.append((wide * (grad_soft - mean)).astype(BF16))
                    head = pl.ds(pl.multiple_of(g * HALF + h * HEAD_DIM, HEAD_DIM), HEAD_DIM)
                    grad_queries.append(dot(key_t[piece, head, own], grad_scores[h]))
                grad_queries = jnp.concatenate(grad_queries, axis=0)
                grad_n[piece, 0, own, feats] = (grad_queries * SCALE).T.astype(BF16)
                grad_keys = dot(
                    jnp.concatenate(grad_scores, axis=1), by_head(query_n[piece, own, feats], 1)
                )
                grad_n[piece, 1, own, feats] = (grad_keys * SCALE).astype(BF16)
                grad_values = dot(soft, by_head(grad_context_n[own, feats], 1))
                grad_n[piece, 2, own, feats] = grad_values.astype(BF16)

    def context_back(piece, rest):
        grads = dot(rest, weights_t[4 * piece + 3]).astype(BF16)
        grad_context_n[...] = grads
        grad_context_t[...] = grads.T

    def input_back(piece, rows, rest):
        first = 4 * piece
        grad_normed = (
            dot(grad_n[piece, 0], weights_t[first])
            + dot(grad_n[piece, 1], weights_t[first + 1])
            + dot(grad_n[piece, 2], weights_t[first + 2])
        )
        inverse = inverse_norm(rows)
        scaled = rows * inverse
        along = jnp.mean(scaled * grad_normed, axis=-1, keepdims=True)
        return rest.astype(F32) + inverse * (grad_normed - scaled * along)

    def put_part(piece, w, s, product):
        split = product.reshape(N_Y * N_Z, 2, 8, 2 * HALF)
        for c in range(2):
            unit = jnp.concatenate([split[:, c, :, :HALF], split[:, c, :, HALF:]], axis=1)
            parts[piece, c, s, w] = unit.astype(BF16).reshape(N_Y, N_Z, 16, HALF)

    def core_parts(s, output):
        return (s, 3) if output else (s, pl.ds(0, 3))

    def core_sem(piece, s, output):
        return CORE + 4 * piece + 2 * s + output

    def send_core(piece, s, output):
        at = core_parts(s, output)
        start(
            parts.at[(piece, 1 - core) + at],
            got_core.at[(piece,) + at],
            core_sem(piece, s, output),
            peer_core,
        )

    def context_sum(piece, rest):
        for s in range(2):
            put_part(piece, 3, s, dot(context_t[piece], rest[:, 2 * HALF * s : 2 * HALF * (s + 1)]))
            send_core(piece, s, 1)

    def normed_sum(piece, s):
        chunk = slice(2 * HALF * s, 2 * HALF * (s + 1))
        for w in range(3):
            put_part(piece, w, s, dot(normed_t[piece], grad_n[piece, w, :, chunk]))
        send_core(piece, s, 0)

    def sum_core(piece, s):
        for output in (1, 0):
            wait(recv_sem, got_core.at[(piece,) + core_parts(s, output)], core_sem(piece, s, output))
        for w in range(4):
            for j in range(N_Y):
                total = (
                    parts[piece, core, s, w, j].astype(F32) + got_core[piece, s, w, j].astype(F32)
                ).astype(BF16)
                if s == 0:
                    sum_a[piece, w, j] = total
                else:
                    sum_b[piece, j, w] = total
        if s == 0:
            for d in range(1, N_X):
                start(sum_a.at[piece, lax.rem(x + d, N_X)], got_a.at[piece, d - 1], FIRST_X + piece, peers_x[d - 1])
        else:
            for d in range(1, N_Y):
                start(sum_b.at[piece, lax.rem(y + d, N_Y)], got_b.at[piece, d - 1], FIRST_Y + piece, peers_y[d - 1])

    def add_up(own, got, n):
        total = own.astype(F32)
        for d in range(n - 1):
            total += got[d].astype(F32)
        return total

    def sum_first(piece, s):
        if s == 0:
            wait(recv_sem, got_a.at[piece], FIRST_X + piece)
            sum_a2[piece] = add_up(sum_a[piece, x], [got_a[piece, d] for d in range(N_X - 1)], N_X).astype(BF16)
            for d in range(1, N_Y):
                start(sum_a2.at[piece, lax.rem(y + d, N_Y)], got_a2.at[piece, d - 1], SECOND_Y + piece, peers_y[d - 1])
        else:
            wait(recv_sem, got_b.at[piece], FIRST_Y + piece)
            sum_b2[piece] = add_up(sum_b[piece, y], [got_b[piece, d] for d in range(N_Y - 1)], N_Y).astype(BF16)
            for d in range(1, N_X):
                start(sum_b2.at[piece, lax.rem(x + d, N_X)], got_b2.at[piece, d - 1], SECOND_X + piece, peers_x[d - 1])

    def sum_second(piece):
        wait(recv_sem, got_a2.at[piece], SECOND_Y + piece)
        last[piece, :, 0] = add_up(sum_a2[piece, y], [got_a2[piece, d] for d in range(N_Y - 1)], N_Y).astype(BF16)
        wait(recv_sem, got_b2.at[piece], SECOND_X + piece)
        last[piece, :, 1] = add_up(sum_b2[piece, x], [got_b2[piece, d] for d in range(N_X - 1)], N_X).astype(BF16)
        for d in range(1, N_Z):
            start(last.at[piece, lax.rem(z + d, N_Z)], got_last.at[piece, d - 1], LAST + piece, peers_z[d - 1])

    def sum_last(piece):
        wait(recv_sem, got_last.at[piece], LAST + piece)
        scaling = (N_X * N_TILE * ROWS) ** (-0.5)
        total = add_up(last[piece, z], [got_last[piece, d] for d in range(N_Z - 1)], N_Z) * scaling
        for s in range(2):
            for half in range(2):
                column = (2 * s + half) * HALF
                weight_out[piece, :, column : column + HALF] = total[s, 8 * half : 8 * half + 8]

    loads[0].wait()
    loads[1].wait()
    project(SPATIAL, blocks[...].astype(F32))

    lane = iota((1, HALF), 1)
    for i in range(2, 5):
        loads[i].wait()
    usable = iota((1, 2), 1) < count[:, 0:1]
    tags = jnp.where(usable, position[...] * FRAMES + frame[...], -1)
    tag_out[...] = jnp.where(lane < N_TILE, tags[:, 0:1], tags[:, 1:2])
    tag_in[t] = tag_out[...]
    pl.semaphore_wait(barrier, N_TILE - 1 + N_X - 1)
    send_all(lambda to: tag_out, tag_in, TAGS)

    attend(SPATIAL)
    loads[5].wait()
    states = blocks[...].astype(F32) + dot_tn(context_t[SPATIAL], weights[3])
    for s in range(2):
        for k in range(4):
            spread[pl.ds(4 * s + k, HALF, stride=8), :] = states[
                s * HALF : (s + 1) * HALF, k * HALF : (k + 1) * HALF
            ]
    box_out[0] = spread[...].astype(BF16).reshape(N_TILE, 16, HALF)
    box_in[0, t] = box_out[0, t]
    send_all(lambda to: box_out.at[0, to], box_in.at[0], STATES)

    for w in range(8):
        weights_t[w] = weights[w].T
    normed_t[SPATIAL] = normed_n[SPATIAL].T
    key_t[SPATIAL] = key_n[SPATIAL].T

    wait(recv_sem, tag_in.at[pl.ds(0, N_TILE - 1)], TAGS)
    entry = iota((N_TILE, HALF), 1)
    placing = jnp.concatenate(
        [
            jnp.where(tag_in[:, 0, N_TILE * s : N_TILE * s + 1] == entry, 1.0, 0.0)
            for s in range(2)
        ],
        axis=0,
    ).astype(BF16)
    active = dot_tn(placing, jnp.ones((HALF, HALF), BF16))
    key_row, query_row = iota((HALF, HALF), 0), iota((HALF, HALF), 1)
    seen = (key_row // FRAMES == query_row // FRAMES) & (key_row <= query_row)
    mask[...] = jnp.where(seen, active, 0.0)
    active_wide = jnp.concatenate([active] * 4, axis=1) > 0.5
    loads[6].wait()
    rest = jnp.concatenate(
        [jnp.where(active_wide, cot[:, j, :].astype(F32), 0.0) for j in range(2)], axis=0
    ).astype(BF16)
    context_back(TEMPORAL, rest)

    wait(recv_sem, box_in.at[0, pl.ds(0, N_TILE - 1)], STATES)
    spread[...] = box_in[0].reshape(N_TILE * 16, HALF).astype(F32)
    for j in range(2):
        rows = jnp.concatenate(
            [
                jnp.concatenate(
                    [spread[pl.ds(8 * j + 4 * s + k, N_TILE, stride=16), :] for k in range(4)], axis=1
                )
                for s in range(2)
            ],
            axis=0,
        ).astype(BF16)
        grid[j * HALF : (j + 1) * HALF] = dot_tn(placing, rows)

    project(TEMPORAL, grid[...])
    key_t[TEMPORAL] = key_n[TEMPORAL].T
    attend(TEMPORAL)
    attend_back(TEMPORAL, 0, HEADS // GROUP)
    grid_grad = input_back(TEMPORAL, grid[...], rest).astype(BF16)
    for j in range(2):
        back = dot(placing, grid_grad[j * HALF : (j + 1) * HALF])
        for s in range(2):
            for k in range(4):
                spread[pl.ds(8 * j + 4 * s + k, N_TILE, stride=16), :] = back[
                    s * N_TILE : (s + 1) * N_TILE, k * HALF : (k + 1) * HALF
                ]
    box_out[1] = spread[...].astype(BF16).reshape(N_TILE, 16, HALF)
    box_in[1, t] = box_out[1, t]
    send_all(lambda to: box_out.at[1, to], box_in.at[1], GRADS)

    context_sum(TEMPORAL, rest)
    normed_t[TEMPORAL] = normed_n[TEMPORAL].T
    normed_sum(TEMPORAL, 0)
    normed_sum(TEMPORAL, 1)
    temporal = grid[...] + dot_tn(context_t[TEMPORAL], weights[7])
    for j in range(2):
        mixed_out[:, j, :] = jnp.where(active_wide, temporal[j * HALF : (j + 1) * HALF], 0.0).astype(BF16)
    stores[0].start()
    sum_core(TEMPORAL, 0)
    sum_core(TEMPORAL, 1)

    wait(recv_sem, box_in.at[1, pl.ds(0, N_TILE - 1)], GRADS)
    spread[...] = box_in[1].reshape(N_TILE * 16, HALF).astype(F32)
    rest = jnp.concatenate(
        [
            jnp.concatenate([spread[pl.ds(4 * s + k, HALF, stride=8), :] for k in range(4)], axis=1)
            for s in range(2)
        ],
        axis=0,
    ).astype(BF16)
    context_sum(SPATIAL, rest)
    context_back(SPATIAL, rest)
    attend_back(SPATIAL, 0, 2)
    normed_sum(SPATIAL, 0)
    sum_first(TEMPORAL, 0)
    sum_first(TEMPORAL, 1)
    attend_back(SPATIAL, 2, 4)
    normed_sum(SPATIAL, 1)
    sum_core(SPATIAL, 0)
    sum_second(TEMPORAL)
    sum_core(SPATIAL, 1)
    grad_out[...] = input_back(SPATIAL, blocks[...].astype(F32), rest).astype(BF16)
    stores[1].start()
    sum_first(SPATIAL, 0)
    sum_first(SPATIAL, 1)
    sum_last(TEMPORAL)
    sum_second(SPATIAL)
    sum_last(SPATIAL)
    stores[2].start()

    wait(send_sem, tag_in.at[pl.ds(0, N_TILE - 1)], TAGS)
    wait(send_sem, box_in.at[0, pl.ds(0, N_TILE - 1)], STATES)
    wait(send_sem, box_in.at[1, pl.ds(0, N_TILE - 1)], GRADS)
    for piece in range(2):
        for s in range(2):
            for output in range(2):
                wait(send_sem, got_core.at[(piece,) + core_parts(s, output)], core_sem(piece, s, output))
        wait(send_sem, got_a.at[piece], FIRST_X + piece)
        wait(send_sem, got_b.at[piece], FIRST_Y + piece)
        wait(send_sem, got_a2.at[piece], SECOND_Y + piece)
        wait(send_sem, got_b2.at[piece], SECOND_X + piece)
        wait(send_sem, got_last.at[piece], LAST + piece)
    for store in stores:
        store.wait()


def hand_over(*refs):
    sources, targets, held, sem_in, sem_out = refs[:3], refs[3:6], refs[6:9], refs[9], refs[10]
    loads = [pltpu.make_async_copy(sources[i], held[i], sem_in.at[i]) for i in range(3)]
    stores = [pltpu.make_async_copy(held[i], targets[i], sem_out.at[i]) for i in range(3)]
    for load in loads:
        load.start()
    for load, store in zip(loads, stores):
        load.wait()
        store.start()
    for store in stores:
        store.wait()


def body(blocks, block_position, block_frame, block_count, weights, cotangent):
    unit = (16, HALF)
    pair = (2, ROWS, WIDTH)
    turned = (2, WIDTH, ROWS)
    hbm = pl.BlockSpec(memory_space=pltpu.HBM)
    out_shape = (
        jax.ShapeDtypeStruct((HALF, 2, WIDTH), BF16),
        jax.ShapeDtypeStruct((ROWS, WIDTH), BF16),
        jax.ShapeDtypeStruct((2, 8, WIDTH), F32),
    )
    results = pl.pallas_call(
        kernel,
        out_shape=out_shape,
        in_specs=[hbm] * 6,
        out_specs=(hbm, hbm, hbm),
        scratch_shapes=[
            pltpu.VMEM((HALF, 2, WIDTH), BF16),
            pltpu.VMEM((ROWS, WIDTH), BF16),
            pltpu.VMEM((2, 8, WIDTH), F32),
            pltpu.VMEM((1, 2), jnp.int32),
            pltpu.VMEM((1, 2), jnp.int32),
            pltpu.VMEM((1, 1), jnp.int32),
            pltpu.VMEM((ROWS, WIDTH), BF16),
            pltpu.VMEM((8, WIDTH, WIDTH), BF16),
            pltpu.VMEM((8, WIDTH, WIDTH), BF16),
            pltpu.VMEM((HALF, 2, WIDTH), BF16),
            pltpu.VMEM((HALF, HALF), F32),
            pltpu.VMEM((1, HALF), jnp.int32),
            pltpu.VMEM((N_TILE, 1, HALF), jnp.int32),
            pltpu.VMEM((N_TILE * 16, HALF), F32),
            pltpu.VMEM((2, N_TILE) + unit, BF16),
            pltpu.VMEM((2, N_TILE) + unit, BF16),
            pltpu.VMEM(pair, BF16),
            pltpu.VMEM(turned, BF16),
            pltpu.VMEM(pair, BF16),
            pltpu.VMEM((WIDTH, ROWS), BF16),
            pltpu.VMEM(pair, BF16),
            pltpu.VMEM(turned, BF16),
            pltpu.VMEM(pair, BF16),
            pltpu.VMEM((WIDTH, ROWS), BF16),
            pltpu.VMEM(turned, BF16),
            pltpu.VMEM((2, HEADS // GROUP, 2, HALF, GROUP * HALF), BF16),
            pltpu.VMEM((ROWS, WIDTH), BF16),
            pltpu.VMEM((WIDTH, ROWS), BF16),
            pltpu.VMEM((2, 3, ROWS, WIDTH), BF16),
            pltpu.VMEM((ROWS, WIDTH), F32),
            pltpu.VMEM((2, 2, 2, 4, N_Y, N_Z) + unit, BF16),
            pltpu.VMEM((2, 2, 4, N_Y, N_Z) + unit, BF16),
            pltpu.VMEM((2, N_X, N_Y, N_Z) + unit, BF16),
            pltpu.VMEM((2, N_Y, N_X, N_Z) + unit, BF16),
            pltpu.VMEM((2, N_X - 1, N_Y, N_Z) + unit, BF16),
            pltpu.VMEM((2, N_Y - 1, N_X, N_Z) + unit, BF16),
            pltpu.VMEM((2, N_Y, N_Z) + unit, BF16),
            pltpu.VMEM((2, N_X, N_Z) + unit, BF16),
            pltpu.VMEM((2, N_Y - 1, N_Z) + unit, BF16),
            pltpu.VMEM((2, N_X - 1, N_Z) + unit, BF16),
            pltpu.VMEM((2, N_Z, 2) + unit, BF16),
            pltpu.VMEM((2, N_Z - 1, 2) + unit, BF16),
            pltpu.SemaphoreType.DMA((7,)),
            pltpu.SemaphoreType.DMA((3,)),
            pltpu.SemaphoreType.DMA((N_SEM,)),
            pltpu.SemaphoreType.DMA((N_SEM,)),
        ],
        compiler_params=pltpu.CompilerParams(
            collective_id=0, has_side_effects=True, vmem_limit_bytes=62 * 1024 * 1024
        ),
    )(
        block_position,
        block_frame,
        block_count,
        blocks.reshape(ROWS, WIDTH),
        weights,
        cotangent.reshape(HALF, 2, WIDTH),
    )
    mixed, input_grad, weight_grad = pl.pallas_call(
        hand_over,
        out_shape=out_shape,
        in_specs=[hbm] * 3,
        out_specs=(hbm, hbm, hbm),
        scratch_shapes=[pltpu.VMEM(leaf.shape, leaf.dtype) for leaf in out_shape]
        + [pltpu.SemaphoreType.DMA((3,))] * 2,
        compiler_params=pltpu.CompilerParams(vmem_limit_bytes=62 * 1024 * 1024),
        name="hand_over",
    )(*results)
    return mixed.reshape(cotangent.shape), input_grad.reshape(blocks.shape), weight_grad


def solution(mesh):
    return jax.shard_map(
        body,
        mesh=mesh,
        in_specs=(
            P("scene", "tile", None, None),
            P("scene", "tile"),
            P("scene", "tile"),
            P("scene", "tile"),
            P(),
            P("scene", None, None, "tile", None),
        ),
        out_specs=(
            P("scene", None, None, "tile", None),
            P("scene", "tile", None, None),
            P(None, ("scene", "tile"), None),
        ),
        check_vma=False,
    )
```

```python
import functools

import jax
import jax.numpy as jnp
from jax import lax
from jax.experimental import pallas as pl
from jax.experimental.pallas import tpu as pltpu
from jax.sharding import PartitionSpec as P

MESH = pl.DeviceIdType.MESH
N_X, N_Y, N_Z, N_TILE = 4, 4, 8, 64
HEADS, HEAD_DIM = 16, 32
WIDTH, ROWS, HALF = 512, 256, 128
FRAMES = 8
GROUP = 4
EPSILON = 1e-06
SPATIAL, TEMPORAL = 0, 1
BF16, F32 = jnp.bfloat16, jnp.float32
EXP2_SCALE = HEAD_DIM ** (-0.5) * 1.4426950408889634
SCALE = HEAD_DIM ** (-0.5)
TAGS, STATES, GRADS, CORE, FIRST, SECOND, LAST = 0, 1, 2, 3, 11, 19, 27
N_SEM = 29
N_GROUP = HEADS // GROUP
N_PAIR = N_Z // 2


def dot(left, right):
    return jnp.dot(left, right, preferred_element_type=F32)


def dot_tn(left, right):
    return lax.dot_general(left, right, (((0,), (0,)), ((), ())), preferred_element_type=F32)


def dot_nt(left, right):
    return lax.dot_general(left, right, (((1,), (1,)), ((), ())), preferred_element_type=F32)


def iota(shape, axis):
    return lax.broadcasted_iota(jnp.int32, shape, axis)


def tile_index(y, z, core):
    return (y * N_Z + z) * 2 + core


def inverse_norm(rows):
    return lax.rsqrt(jnp.mean(rows * rows, axis=-1, keepdims=True) + EPSILON)


def kernel(
    position_in,
    frame_in,
    count_in,
    blocks_in,
    weights_in,
    cot_in,
    mixed_to,
    grad_to,
    weight_to,
    mixed_out,
    grad_out,
    weight_out,
    position,
    frame,
    count,
    blocks,
    weights,
    weights_t,
    cot,
    mask,
    tag_out,
    tag_in,
    spread,
    box_out,
    box_in,
    normed_n,
    normed_t,
    query_n,
    query_t,
    key_n,
    key_t,
    value_n,
    value_t,
    context_t,
    soft_t,
    grad_context_n,
    grad_context_t,
    grad_n,
    grid,
    parts,
    got_core,
    sum_one,
    got_one,
    sum_two,
    got_two,
    last,
    got_last,
    in_sem,
    out_sem,
    send_sem,
    recv_sem,
):
    loads = [
        pltpu.make_async_copy(source, target, in_sem.at[i])
        for i, (source, target) in enumerate(
            [
                (blocks_in, blocks),
                (weights_in.at[pl.ds(0, 3)], weights.at[pl.ds(0, 3)]),
                (position_in, position),
                (frame_in, frame),
                (count_in, count),
                (weights_in.at[pl.ds(3, 5)], weights.at[pl.ds(3, 5)]),
                (cot_in, cot),
            ]
        )
    ]
    for load in loads:
        load.start()
    stores = [
        pltpu.make_async_copy(source, target, out_sem.at[i])
        for i, (source, target) in enumerate(
            [(mixed_out, mixed_to), (grad_out, grad_to), (weight_out, weight_to)]
        )
    ]

    x = lax.axis_index("scene")
    t = lax.axis_index("tile")
    core, z, y = lax.rem(t, 2), lax.rem(t // 2, N_Z), t // (2 * N_Z)
    peer_core = (x, tile_index(y, z, 1 - core))
    peers_x = [(lax.rem(x + d, N_X), t) for d in range(1, N_X)]
    peers_y = [(x, tile_index(lax.rem(y + d, N_Y), z, core)) for d in range(1, N_Y)]
    peers_z = [(x, tile_index(y, lax.rem(z + d, N_Z), core)) for d in range(1, N_Z)]

    barrier = pltpu.get_barrier_semaphore()

    @pl.loop(1, N_TILE)
    def _(d):
        pl.semaphore_signal(
            barrier, inc=1, device_id=(x, lax.rem(t + d, N_TILE)), device_id_type=MESH
        )

    for peer in peers_x:
        pl.semaphore_signal(barrier, inc=1, device_id=peer, device_id_type=MESH)

    def start(source, target, sem, peer):
        pltpu.make_async_remote_copy(
            src_ref=source,
            dst_ref=target,
            send_sem=send_sem.at[sem],
            recv_sem=recv_sem.at[sem],
            device_id=peer,
            device_id_type=MESH,
        ).start()

    def wait(sems, ref, sem):
        pltpu.make_async_copy(ref, ref, sems.at[sem]).wait()

    def send_all(outgoing, incoming, sem):
        @pl.loop(1, N_TILE)
        def _(d):
            to = lax.rem(t + d, N_TILE)
            start(outgoing(to), incoming.at[t], sem, (x, to))

    def project(piece, rows):
        scaled = (rows * inverse_norm(rows)).astype(BF16)
        normed_n[piece] = scaled
        first = 4 * piece
        queries = dot(scaled, weights[first]).astype(BF16)
        query_n[piece] = queries
        query_t[...] = queries.T
        key_n[piece] = dot(scaled, weights[first + 1]).astype(BF16)
        values = dot(scaled, weights[first + 2]).astype(BF16)
        value_n[piece] = values
        value_t[...] = values.T

    def one_head(rows, h, axis):
        owner = iota((HALF, HALF), axis) // HEAD_DIM
        return jnp.where(owner == h, rows, jnp.zeros_like(rows))

    def by_head(rows, axis):
        return jnp.concatenate([one_head(rows, h, axis) for h in range(GROUP)], axis=1 - axis)

    def attend(piece):
        for g in range(N_GROUP):
            feats = slice(g * HALF, (g + 1) * HALF)
            for b in range(2):
                own = slice(b * HALF, (b + 1) * HALF)
                queries = query_t[feats, own]
                keys = key_n[piece, own, feats]
                for h in range(GROUP):
                    scores = dot(keys, one_head(queries, h, 0))
                    if piece == TEMPORAL:
                        scores = jnp.where(mask[...] > 0.5, scores, -1e30)
                    top = jnp.max(scores, axis=0, keepdims=True)
                    powers = jnp.exp2((scores - top) * EXP2_SCALE)
                    share = 1.0 / jnp.sum(powers, axis=0, keepdims=True)
                    soft = (powers * share).astype(BF16)
                    soft_t[piece, g, b, :, h * HALF : (h + 1) * HALF] = soft
                    head = slice(g * HALF + h * HEAD_DIM, g * HALF + (h + 1) * HEAD_DIM)
                    context_t[piece, head, own] = dot(value_t[head, own], soft).astype(BF16)

    def attend_back(piece, lower, upper):
        for g in range(lower, upper):
            feats = slice(g * HALF, (g + 1) * HALF)
            for b in range(2):
                own = slice(b * HALF, (b + 1) * HALF)
                grads_t = grad_context_t[feats, own]
                values = value_n[piece, own, feats]
                soft = soft_t[piece, g, b]
                grad_scores, grad_queries = [], []
                for h in range(GROUP):
                    wide = soft[:, h * HALF : (h + 1) * HALF].astype(F32)
                    grad_soft = dot(values, one_head(grads_t, h, 0))
                    mean = jnp.sum(wide * grad_soft, axis=0, keepdims=True)
                    grad_scores.append((wide * (grad_soft - mean)).astype(BF16))
                    head = slice(g * HALF + h * HEAD_DIM, g * HALF + (h + 1) * HEAD_DIM)
                    grad_queries.append(dot(key_t[piece, head, own], grad_scores[h]))
                grad_queries = jnp.concatenate(grad_queries, axis=0)
                grad_n[piece, 0, own, feats] = (grad_queries * SCALE).T.astype(BF16)
                grad_keys = dot(
                    jnp.concatenate(grad_scores, axis=1), by_head(query_n[piece, own, feats], 1)
                )
                grad_n[piece, 1, own, feats] = (grad_keys * SCALE).astype(BF16)
                grad_values = dot(soft, by_head(grad_context_n[own, feats], 1))
                grad_n[piece, 2, own, feats] = grad_values.astype(BF16)

    def context_back(piece, rest):
        grads = dot(rest, weights_t[4 * piece + 3]).astype(BF16)
        grad_context_n[...] = grads
        grad_context_t[...] = grads.T

    def input_back(piece, rows, rest):
        first = 4 * piece
        grad_normed = (
            dot(grad_n[piece, 0], weights_t[first])
            + dot(grad_n[piece, 1], weights_t[first + 1])
            + dot(grad_n[piece, 2], weights_t[first + 2])
        )
        inverse = inverse_norm(rows)
        scaled = rows * inverse
        along = jnp.mean(scaled * grad_normed, axis=-1, keepdims=True)
        return rest.astype(F32) + inverse * (grad_normed - scaled * along)

    def put_part(piece, g, w, product):
        split = product.reshape(N_Y * N_Z, 2, 8, HALF)
        for c in range(2):
            parts[piece, c, g, w] = (
                split[:, c].reshape(N_Y, N_PAIR, 16, HALF).astype(BF16)
            )

    def context_sum(piece, rest):
        product = dot(context_t[piece], rest)
        for g in range(N_GROUP):
            put_part(piece, g, 3, product[:, g * HALF : (g + 1) * HALF])

    def normed_sum(piece, g):
        chunk = slice(g * HALF, (g + 1) * HALF)
        grads = jnp.concatenate([grad_n[piece, w, :, chunk] for w in range(3)], axis=1)
        product = dot(normed_t[piece], grads)
        for w in range(3):
            put_part(piece, g, w, product[:, w * HALF : (w + 1) * HALF])
        start(parts.at[piece, 1 - core, g], got_core.at[piece, g], CORE + 4 * piece + g, peer_core)

    def add_up(own, got, n):
        total = own.astype(F32)
        for d in range(n - 1):
            total += got[d].astype(F32)
        return total

    def send_one(piece, g):
        me, peers = (x, peers_x) if g % 2 == 0 else (y, peers_y)
        for d in range(1, 4):
            start(sum_one.at[piece, g, lax.rem(me + d, 4)], got_one.at[piece, g, d - 1], FIRST + 4 * piece + g, peers[d - 1])

    def sum_core(piece, g):
        wait(recv_sem, got_core.at[piece, g], CORE + 4 * piece + g)
        for w in range(4):
            for j in range(N_Y):
                at = (w, j) if g % 2 == 0 else (j, w)
                sum_one[(piece, g) + at] = (
                    parts[piece, core, g, w, j].astype(F32) + got_core[piece, g, w, j].astype(F32)
                ).astype(BF16)
        send_one(piece, g)

    def sum_first(piece, g):
        first, second, peers = (x, y, peers_y) if g % 2 == 0 else (y, x, peers_x)
        wait(recv_sem, got_one.at[piece, g], FIRST + 4 * piece + g)
        sum_two[piece, g] = add_up(sum_one[piece, g, first], [got_one[piece, g, d] for d in range(3)], 4).astype(BF16)
        for d in range(1, 4):
            start(sum_two.at[piece, g, lax.rem(second + d, 4)], got_two.at[piece, g, d - 1], SECOND + 4 * piece + g, peers[d - 1])

    def sum_second(piece):
        for s in range(2):
            halves = []
            for g in (2 * s, 2 * s + 1):
                second = y if g % 2 == 0 else x
                wait(recv_sem, got_two.at[piece, g], SECOND + 4 * piece + g)
                total = add_up(sum_two[piece, g, second], [got_two[piece, g, d] for d in range(3)], 4)
                halves.append(total.reshape(N_Z, 8, HALF))
            last[piece, :, s] = jnp.concatenate(halves, axis=1).astype(BF16)
        for d in range(1, N_Z):
            start(last.at[piece, lax.rem(z + d, N_Z)], got_last.at[piece, d - 1], LAST + piece, peers_z[d - 1])

    def sum_last(piece):
        wait(recv_sem, got_last.at[piece], LAST + piece)
        scaling = (N_X * N_TILE * ROWS) ** (-0.5)
        total = add_up(last[piece, z], [got_last[piece, d] for d in range(N_Z - 1)], N_Z) * scaling
        for s in range(2):
            for half in range(2):
                column = (2 * s + half) * HALF
                weight_out[piece, :, column : column + HALF] = total[s, 8 * half : 8 * half + 8]

    loads[0].wait()
    loads[1].wait()
    project(SPATIAL, blocks[...].astype(F32))

    lane = iota((1, HALF), 1)
    for i in range(2, 5):
        loads[i].wait()
    usable = iota((1, 2), 1) < count[:, 0:1]
    tags = jnp.where(usable, position[...] * FRAMES + frame[...], -1)
    tag_out[...] = jnp.where(lane < N_TILE, tags[:, 0:1], tags[:, 1:2])
    tag_in[t] = tag_out[...]
    pl.semaphore_wait(barrier, N_TILE - 1 + N_X - 1)
    send_all(lambda to: tag_out, tag_in, TAGS)

    attend(SPATIAL)
    loads[5].wait()
    states = blocks[...].astype(F32) + dot_tn(context_t[SPATIAL], weights[3])
    for s in range(2):
        for k in range(4):
            spread[pl.ds(4 * s + k, HALF, stride=8), :] = states[
                s * HALF : (s + 1) * HALF, k * HALF : (k + 1) * HALF
            ]
    box_out[0] = spread[...].astype(BF16).reshape(N_TILE, 16, HALF)
    box_in[0, t] = box_out[0, t]
    send_all(lambda to: box_out.at[0, to], box_in.at[0], STATES)

    for w in range(8):
        weights_t[w] = weights[w].T
    normed_t[SPATIAL] = normed_n[SPATIAL].T
    key_t[SPATIAL] = key_n[SPATIAL].T

    wait(recv_sem, tag_in.at[pl.ds(0, N_TILE - 1)], TAGS)
    entry = iota((N_TILE, HALF), 1)
    placing = jnp.concatenate(
        [
            jnp.where(tag_in[:, 0, N_TILE * s : N_TILE * s + 1] == entry, 1.0, 0.0)
            for s in range(2)
        ],
        axis=0,
    ).astype(BF16)
    active = dot_tn(placing, jnp.ones((HALF, HALF), BF16))
    key_row, query_row = iota((HALF, HALF), 0), iota((HALF, HALF), 1)
    seen = (key_row // FRAMES == query_row // FRAMES) & (key_row <= query_row)
    mask[...] = jnp.where(seen, active, 0.0)
    active_wide = jnp.concatenate([active] * 4, axis=1) > 0.5
    loads[6].wait()
    rest = jnp.concatenate(
        [jnp.where(active_wide, cot[:, j, :].astype(F32), 0.0) for j in range(2)], axis=0
    ).astype(BF16)
    context_back(TEMPORAL, rest)

    wait(recv_sem, box_in.at[0, pl.ds(0, N_TILE - 1)], STATES)
    spread[...] = box_in[0].reshape(N_TILE * 16, HALF).astype(F32)
    for j in range(2):
        rows = jnp.concatenate(
            [
                jnp.concatenate(
                    [spread[pl.ds(8 * j + 4 * s + k, N_TILE, stride=16), :] for k in range(4)], axis=1
                )
                for s in range(2)
            ],
            axis=0,
        ).astype(BF16)
        grid[j * HALF : (j + 1) * HALF] = dot_tn(placing, rows)

    project(TEMPORAL, grid[...])
    key_t[TEMPORAL] = key_n[TEMPORAL].T
    attend(TEMPORAL)
    attend_back(TEMPORAL, 0, N_GROUP)
    grid_grad = input_back(TEMPORAL, grid[...], rest).astype(BF16)
    for j in range(2):
        back = dot(placing, grid_grad[j * HALF : (j + 1) * HALF])
        for s in range(2):
            for k in range(4):
                spread[pl.ds(8 * j + 4 * s + k, N_TILE, stride=16), :] = back[
                    s * N_TILE : (s + 1) * N_TILE, k * HALF : (k + 1) * HALF
                ]
    box_out[1] = spread[...].astype(BF16).reshape(N_TILE, 16, HALF)
    box_in[1, t] = box_out[1, t]
    send_all(lambda to: box_out.at[1, to], box_in.at[1], GRADS)

    context_sum(TEMPORAL, rest)
    normed_t[TEMPORAL] = normed_n[TEMPORAL].T
    for g in range(N_GROUP):
        normed_sum(TEMPORAL, g)
    temporal = grid[...] + dot_tn(context_t[TEMPORAL], weights[7])
    for j in range(2):
        mixed_out[:, j, :] = jnp.where(active_wide, temporal[j * HALF : (j + 1) * HALF], 0.0).astype(BF16)
    stores[0].start()
    for g in range(N_GROUP):
        sum_core(TEMPORAL, g)

    wait(recv_sem, box_in.at[1, pl.ds(0, N_TILE - 1)], GRADS)
    spread[...] = box_in[1].reshape(N_TILE * 16, HALF).astype(F32)
    rest = jnp.concatenate(
        [
            jnp.concatenate([spread[pl.ds(4 * s + k, HALF, stride=8), :] for k in range(4)], axis=1)
            for s in range(2)
        ],
        axis=0,
    ).astype(BF16)
    context_sum(SPATIAL, rest)
    context_back(SPATIAL, rest)
    for g in range(N_GROUP):
        attend_back(SPATIAL, g, g + 1)
        normed_sum(SPATIAL, g)
        if g > 0:
            sum_core(SPATIAL, g - 1)
        if g == 1:
            for group in range(N_GROUP):
                sum_first(TEMPORAL, group)
    input_grad = input_back(SPATIAL, blocks[...].astype(F32), rest).astype(BF16)
    sum_core(SPATIAL, N_GROUP - 1)
    grad_out[...] = input_grad
    stores[1].start()
    sum_second(TEMPORAL)
    for g in range(N_GROUP):
        sum_first(SPATIAL, g)
    sum_last(TEMPORAL)
    sum_second(SPATIAL)
    sum_last(SPATIAL)
    stores[2].start()

    wait(send_sem, tag_in.at[pl.ds(0, N_TILE - 1)], TAGS)
    wait(send_sem, box_in.at[0, pl.ds(0, N_TILE - 1)], STATES)
    wait(send_sem, box_in.at[1, pl.ds(0, N_TILE - 1)], GRADS)
    for piece in range(2):
        for g in range(N_GROUP):
            wait(send_sem, got_core.at[piece, g], CORE + 4 * piece + g)
            wait(send_sem, got_one.at[piece, g], FIRST + 4 * piece + g)
            wait(send_sem, got_two.at[piece, g], SECOND + 4 * piece + g)
        wait(send_sem, got_last.at[piece], LAST + piece)
    for store in stores:
        store.wait()


def hand_over(*refs):
    sources, targets, held, sem_in, sem_out = refs[:3], refs[3:6], refs[6:9], refs[9], refs[10]
    loads = [pltpu.make_async_copy(sources[i], held[i], sem_in.at[i]) for i in range(3)]
    stores = [pltpu.make_async_copy(held[i], targets[i], sem_out.at[i]) for i in range(3)]
    for load in loads:
        load.start()
    for load, store in zip(loads, stores):
        load.wait()
        store.start()
    for store in stores:
        store.wait()


def body(blocks, block_position, block_frame, block_count, weights, cotangent):
    unit = (16, HALF)
    pair = (2, ROWS, WIDTH)
    turned = (2, WIDTH, ROWS)
    hbm = pl.BlockSpec(memory_space=pltpu.HBM)
    out_shape = (
        jax.ShapeDtypeStruct((HALF, 2, WIDTH), BF16),
        jax.ShapeDtypeStruct((ROWS, WIDTH), BF16),
        jax.ShapeDtypeStruct((2, 8, WIDTH), F32),
    )
    results = pl.pallas_call(
        kernel,
        out_shape=out_shape,
        in_specs=[hbm] * 6,
        out_specs=(hbm, hbm, hbm),
        scratch_shapes=[
            pltpu.VMEM((HALF, 2, WIDTH), BF16),
            pltpu.VMEM((ROWS, WIDTH), BF16),
            pltpu.VMEM((2, 8, WIDTH), F32),
            pltpu.VMEM((1, 2), jnp.int32),
            pltpu.VMEM((1, 2), jnp.int32),
            pltpu.VMEM((1, 1), jnp.int32),
            pltpu.VMEM((ROWS, WIDTH), BF16),
            pltpu.VMEM((8, WIDTH, WIDTH), BF16),
            pltpu.VMEM((8, WIDTH, WIDTH), BF16),
            pltpu.VMEM((HALF, 2, WIDTH), BF16),
            pltpu.VMEM((HALF, HALF), F32),
            pltpu.VMEM((1, HALF), jnp.int32),
            pltpu.VMEM((N_TILE, 1, HALF), jnp.int32),
            pltpu.VMEM((N_TILE * 16, HALF), F32),
            pltpu.VMEM((2, N_TILE) + unit, BF16),
            pltpu.VMEM((2, N_TILE) + unit, BF16),
            pltpu.VMEM(pair, BF16),
            pltpu.VMEM(turned, BF16),
            pltpu.VMEM(pair, BF16),
            pltpu.VMEM((WIDTH, ROWS), BF16),
            pltpu.VMEM(pair, BF16),
            pltpu.VMEM(turned, BF16),
            pltpu.VMEM(pair, BF16),
            pltpu.VMEM((WIDTH, ROWS), BF16),
            pltpu.VMEM(turned, BF16),
            pltpu.VMEM((2, N_GROUP, 2, HALF, GROUP * HALF), BF16),
            pltpu.VMEM((ROWS, WIDTH), BF16),
            pltpu.VMEM((WIDTH, ROWS), BF16),
            pltpu.VMEM((2, 3, ROWS, WIDTH), BF16),
            pltpu.VMEM((ROWS, WIDTH), F32),
            pltpu.VMEM((2, 2, N_GROUP, 4, N_Y, N_PAIR) + unit, BF16),
            pltpu.VMEM((2, N_GROUP, 4, N_Y, N_PAIR) + unit, BF16),
            pltpu.VMEM((2, N_GROUP, 4, 4, N_PAIR) + unit, BF16),
            pltpu.VMEM((2, N_GROUP, 3, 4, N_PAIR) + unit, BF16),
            pltpu.VMEM((2, N_GROUP, 4, N_PAIR) + unit, BF16),
            pltpu.VMEM((2, N_GROUP, 3, N_PAIR) + unit, BF16),
            pltpu.VMEM((2, N_Z, 2) + unit, BF16),
            pltpu.VMEM((2, N_Z - 1, 2) + unit, BF16),
            pltpu.SemaphoreType.DMA((7,)),
            pltpu.SemaphoreType.DMA((3,)),
            pltpu.SemaphoreType.DMA((N_SEM,)),
            pltpu.SemaphoreType.DMA((N_SEM,)),
        ],
        compiler_params=pltpu.CompilerParams(
            collective_id=0, has_side_effects=True, vmem_limit_bytes=62 * 1024 * 1024
        ),
    )(
        block_position,
        block_frame,
        block_count,
        blocks.reshape(ROWS, WIDTH),
        weights,
        cotangent.reshape(HALF, 2, WIDTH),
    )
    mixed, input_grad, weight_grad = pl.pallas_call(
        hand_over,
        out_shape=out_shape,
        in_specs=[hbm] * 3,
        out_specs=(hbm, hbm, hbm),
        scratch_shapes=[pltpu.VMEM(leaf.shape, leaf.dtype) for leaf in out_shape]
        + [pltpu.SemaphoreType.DMA((3,))] * 2,
        compiler_params=pltpu.CompilerParams(vmem_limit_bytes=62 * 1024 * 1024),
        name="hand_over",
    )(*results)
    return mixed.reshape(cotangent.shape), input_grad.reshape(blocks.shape), weight_grad


def solution(mesh):
    return jax.shard_map(
        body,
        mesh=mesh,
        in_specs=(
            P("scene", "tile", None, None),
            P("scene", "tile"),
            P("scene", "tile"),
            P("scene", "tile"),
            P(),
            P("scene", None, None, "tile", None),
        ),
        out_specs=(
            P("scene", None, None, "tile", None),
            P("scene", "tile", None, None),
            P(None, ("scene", "tile"), None),
        ),
        check_vma=False,
    )
```

```python
import functools

import jax
import jax.numpy as jnp
from jax import lax
from jax.experimental import pallas as pl
from jax.experimental.pallas import tpu as pltpu
from jax.sharding import PartitionSpec as P

MESH = pl.DeviceIdType.MESH
N_X, N_Y, N_Z, N_TILE = 4, 4, 8, 64
HEADS, HEAD_DIM = 16, 32
WIDTH, ROWS, HALF = 512, 256, 128
FRAMES = 8
GROUP = 4
EPSILON = 1e-06
SPATIAL, TEMPORAL = 0, 1
BF16, F32 = jnp.bfloat16, jnp.float32
EXP2_SCALE = HEAD_DIM ** (-0.5) * 1.4426950408889634
SCALE = HEAD_DIM ** (-0.5)
TAGS, STATES, GRADS, CORE, FIRST, SECOND, LAST = 0, 1, 3, 5, 13, 21, 29
N_SEM = 31
N_GROUP = HEADS // GROUP
N_PAIR = N_Z // 2


def dot(left, right):
    return jnp.dot(left, right, preferred_element_type=F32)


def dot_tn(left, right):
    return lax.dot_general(left, right, (((0,), (0,)), ((), ())), preferred_element_type=F32)


def dot_nt(left, right):
    return lax.dot_general(left, right, (((1,), (1,)), ((), ())), preferred_element_type=F32)


def iota(shape, axis):
    return lax.broadcasted_iota(jnp.int32, shape, axis)


def tile_index(y, z, core):
    return (y * N_Z + z) * 2 + core


def inverse_norm(rows):
    return lax.rsqrt(jnp.mean(rows * rows, axis=-1, keepdims=True) + EPSILON)


def kernel(
    position_in,
    frame_in,
    count_in,
    blocks_in,
    weights_in,
    cot_in,
    mixed_to,
    grad_to,
    weight_to,
    mixed_out,
    grad_out,
    weight_out,
    position,
    frame,
    count,
    blocks,
    weights,
    weights_t,
    cot,
    mask,
    tag_out,
    tag_in,
    spread,
    box_out,
    box_in,
    normed_n,
    normed_t,
    query_n,
    query_t,
    key_n,
    key_t,
    value_n,
    value_t,
    context_t,
    soft_t,
    grad_context_n,
    grad_context_t,
    grad_n,
    grid,
    parts,
    got_core,
    sum_one,
    got_one,
    sum_two,
    got_two,
    last,
    got_last,
    in_sem,
    out_sem,
    send_sem,
    recv_sem,
):
    loads = [
        pltpu.make_async_copy(source, target, in_sem.at[i])
        for i, (source, target) in enumerate(
            [
                (blocks_in, blocks),
                (weights_in.at[pl.ds(0, 3)], weights.at[pl.ds(0, 3)]),
                (position_in, position),
                (frame_in, frame),
                (count_in, count),
                (weights_in.at[pl.ds(3, 5)], weights.at[pl.ds(3, 5)]),
                (cot_in, cot),
            ]
        )
    ]
    for load in loads:
        load.start()
    stores = [
        pltpu.make_async_copy(source, target, out_sem.at[i])
        for i, (source, target) in enumerate(
            [(mixed_out, mixed_to), (grad_out, grad_to), (weight_out, weight_to)]
        )
    ]

    x = lax.axis_index("scene")
    t = lax.axis_index("tile")
    core, z, y = lax.rem(t, 2), lax.rem(t // 2, N_Z), t // (2 * N_Z)
    peer_core = (x, tile_index(y, z, 1 - core))
    peers_x = [(lax.rem(x + d, N_X), t) for d in range(1, N_X)]
    peers_y = [(x, tile_index(lax.rem(y + d, N_Y), z, core)) for d in range(1, N_Y)]
    peers_z = [(x, tile_index(y, lax.rem(z + d, N_Z), core)) for d in range(1, N_Z)]

    barrier = pltpu.get_barrier_semaphore()

    for d in range(1, N_TILE):
        pl.semaphore_signal(
            barrier, inc=1, device_id=(x, lax.rem(t + d, N_TILE)), device_id_type=MESH
        )

    for peer in peers_x:
        pl.semaphore_signal(barrier, inc=1, device_id=peer, device_id_type=MESH)

    def start(source, target, sem, peer):
        pltpu.make_async_remote_copy(
            src_ref=source,
            dst_ref=target,
            send_sem=send_sem.at[sem],
            recv_sem=recv_sem.at[sem],
            device_id=peer,
            device_id_type=MESH,
        ).start()

    def wait(sems, ref, sem):
        pltpu.make_async_copy(ref, ref, sems.at[sem]).wait()

    def send_all(outgoing, incoming, sem):
        @pl.loop(1, N_TILE)
        def _(d):
            to = lax.rem(t + d, N_TILE)
            start(outgoing(to), incoming.at[t], sem, (x, to))

    def project(piece, rows, own):
        scaled = (rows * inverse_norm(rows)).astype(BF16)
        normed_n[piece, own] = scaled
        first = 4 * piece
        queries = dot(scaled, weights[first]).astype(BF16)
        query_n[piece, own] = queries
        query_t[:, own] = queries.T
        key_n[piece, own] = dot(scaled, weights[first + 1]).astype(BF16)
        values = dot(scaled, weights[first + 2]).astype(BF16)
        value_n[piece, own] = values
        value_t[:, own] = values.T

    def one_head(rows, h, axis):
        owner = iota((HALF, HALF), axis) // HEAD_DIM
        return jnp.where(owner == h, rows, jnp.zeros_like(rows))

    def by_head(rows, axis):
        return jnp.concatenate([one_head(rows, h, axis) for h in range(GROUP)], axis=1 - axis)

    def attend(piece, lower, upper, halves):
        for g in range(lower, upper):
            feats = slice(g * HALF, (g + 1) * HALF)
            for b in halves:
                own = slice(b * HALF, (b + 1) * HALF)
                queries = query_t[feats, own]
                keys = key_n[piece, own, feats]
                for h in range(GROUP):
                    scores = dot(keys, one_head(queries, h, 0))
                    if piece == TEMPORAL:
                        scores = jnp.where(mask[...] > 0.5, scores, -1e30)
                    top = jnp.max(scores, axis=0, keepdims=True)
                    powers = jnp.exp2((scores - top) * EXP2_SCALE)
                    share = 1.0 / jnp.sum(powers, axis=0, keepdims=True)
                    soft = (powers * share).astype(BF16)
                    soft_t[piece, g, b, :, h * HALF : (h + 1) * HALF] = soft
                    head = slice(g * HALF + h * HEAD_DIM, g * HALF + (h + 1) * HEAD_DIM)
                    context_t[piece, head, own] = dot(value_t[head, own], soft).astype(BF16)

    def attend_back(piece, lower, upper, halves):
        for g in range(lower, upper):
            feats = slice(g * HALF, (g + 1) * HALF)
            for b in halves:
                own = slice(b * HALF, (b + 1) * HALF)
                grads_t = grad_context_t[feats, own]
                values = value_n[piece, own, feats]
                soft = soft_t[piece, g, b]
                grad_scores, grad_queries = [], []
                for h in range(GROUP):
                    wide = soft[:, h * HALF : (h + 1) * HALF].astype(F32)
                    grad_soft = dot(values, one_head(grads_t, h, 0))
                    mean = jnp.sum(wide * grad_soft, axis=0, keepdims=True)
                    grad_scores.append((wide * (grad_soft - mean)).astype(BF16))
                    head = slice(g * HALF + h * HEAD_DIM, g * HALF + (h + 1) * HEAD_DIM)
                    grad_queries.append(dot(key_t[piece, head, own], grad_scores[h]))
                grad_queries = jnp.concatenate(grad_queries, axis=0)
                grad_n[piece, 0, own, feats] = (grad_queries * SCALE).T.astype(BF16)
                grad_keys = dot(
                    jnp.concatenate(grad_scores, axis=1), by_head(query_n[piece, own, feats], 1)
                )
                grad_n[piece, 1, own, feats] = (grad_keys * SCALE).astype(BF16)
                grad_values = dot(soft, by_head(grad_context_n[own, feats], 1))
                grad_n[piece, 2, own, feats] = grad_values.astype(BF16)

    def context_back(piece, rest):
        grads = dot(rest, weights_t[4 * piece + 3]).astype(BF16)
        grad_context_n[...] = grads
        grad_context_t[...] = grads.T

    def normed_back(piece, own):
        first = 4 * piece
        return (
            dot(grad_n[piece, 0, own], weights_t[first])
            + dot(grad_n[piece, 1, own], weights_t[first + 1])
            + dot(grad_n[piece, 2, own], weights_t[first + 2])
        )

    def input_back(rows, rest, grad_normed):
        inverse = inverse_norm(rows)
        scaled = rows * inverse
        along = jnp.mean(scaled * grad_normed, axis=-1, keepdims=True)
        return rest.astype(F32) + inverse * (grad_normed - scaled * along)

    def put_part(piece, g, w, product):
        split = product.reshape(N_Y * N_Z, 2, 8, HALF)
        for c in range(2):
            parts[piece, c, g, w] = (
                split[:, c].reshape(N_Y, N_PAIR, 16, HALF).astype(BF16)
            )

    def context_sum(piece, rest):
        product = dot(context_t[piece], rest)
        for g in range(N_GROUP):
            put_part(piece, g, 3, product[:, g * HALF : (g + 1) * HALF])

    def normed_sum(piece, g):
        chunk = slice(g * HALF, (g + 1) * HALF)
        grads = jnp.concatenate([grad_n[piece, w, :, chunk] for w in range(3)], axis=1)
        product = dot(normed_t[piece], grads)
        for w in range(3):
            put_part(piece, g, w, product[:, w * HALF : (w + 1) * HALF])
        start(parts.at[piece, 1 - core, g], got_core.at[piece, g], CORE + 4 * piece + g, peer_core)

    def add_up(own, got, n):
        total = own.astype(F32)
        for d in range(n - 1):
            total += got[d].astype(F32)
        return total

    def send_one(piece, g):
        me, peers = (x, peers_x) if g % 2 == 0 else (y, peers_y)
        for d in range(1, 4):
            start(sum_one.at[piece, g, lax.rem(me + d, 4)], got_one.at[piece, g, d - 1], FIRST + 4 * piece + g, peers[d - 1])

    def sum_core(piece, g):
        wait(recv_sem, got_core.at[piece, g], CORE + 4 * piece + g)
        for w in range(4):
            for j in range(N_Y):
                at = (w, j) if g % 2 == 0 else (j, w)
                sum_one[(piece, g) + at] = (
                    parts[piece, core, g, w, j].astype(F32) + got_core[piece, g, w, j].astype(F32)
                ).astype(BF16)
        send_one(piece, g)

    def sum_first(piece, g):
        first, second, peers = (x, y, peers_y) if g % 2 == 0 else (y, x, peers_x)
        wait(recv_sem, got_one.at[piece, g], FIRST + 4 * piece + g)
        sum_two[piece, g] = add_up(sum_one[piece, g, first], [got_one[piece, g, d] for d in range(3)], 4).astype(BF16)
        for d in range(1, 4):
            start(sum_two.at[piece, g, lax.rem(second + d, 4)], got_two.at[piece, g, d - 1], SECOND + 4 * piece + g, peers[d - 1])

    def sum_second(piece):
        for s in range(2):
            halves = []
            for g in (2 * s, 2 * s + 1):
                second = y if g % 2 == 0 else x
                wait(recv_sem, got_two.at[piece, g], SECOND + 4 * piece + g)
                total = add_up(sum_two[piece, g, second], [got_two[piece, g, d] for d in range(3)], 4)
                halves.append(total.reshape(N_Z, 8, HALF))
            last[piece, :, s] = jnp.concatenate(halves, axis=1).astype(BF16)
        for d in range(1, N_Z):
            start(last.at[piece, lax.rem(z + d, N_Z)], got_last.at[piece, d - 1], LAST + piece, peers_z[d - 1])

    def sum_last(piece):
        wait(recv_sem, got_last.at[piece], LAST + piece)
        scaling = (N_X * N_TILE * ROWS) ** (-0.5)
        total = add_up(last[piece, z], [got_last[piece, d] for d in range(N_Z - 1)], N_Z) * scaling
        for s in range(2):
            for half in range(2):
                column = (2 * s + half) * HALF
                weight_out[piece, :, column : column + HALF] = total[s, 8 * half : 8 * half + 8]

    loads[0].wait()
    loads[1].wait()
    whole, both = slice(0, ROWS), (0, 1)
    project(SPATIAL, blocks[...].astype(F32), whole)

    attend(SPATIAL, 0, 3, both)
    lane = iota((1, HALF), 1)
    for i in range(2, 5):
        loads[i].wait()
    usable = iota((1, 2), 1) < count[:, 0:1]
    tags = jnp.where(usable, position[...] * FRAMES + frame[...], -1)
    tag_out[...] = jnp.where(lane < N_TILE, tags[:, 0:1], tags[:, 1:2])
    tag_in[t] = tag_out[...]
    pl.semaphore_wait(barrier, N_TILE - 1 + N_X - 1)
    send_all(lambda to: tag_out, tag_in, TAGS)

    attend(SPATIAL, 3, 4, both)
    loads[5].wait()
    states = blocks[...].astype(F32) + dot_tn(context_t[SPATIAL], weights[3])
    for s in range(2):
        for k in range(4):
            spread[pl.ds(4 * s + k, HALF, stride=8), :] = states[
                s * HALF : (s + 1) * HALF, k * HALF : (k + 1) * HALF
            ]
    for j in range(2):
        box_out[0, j] = spread[...].reshape(N_TILE, 2, 8, HALF)[:, j].astype(BF16)
        box_in[0, j, t] = box_out[0, j, t]
        send_all(lambda to: box_out.at[0, j, to], box_in.at[0, j], STATES + j)

    for w in range(8):
        weights_t[w] = weights[w].T
    normed_t[SPATIAL] = normed_n[SPATIAL].T
    key_t[SPATIAL] = key_n[SPATIAL].T

    wait(recv_sem, tag_in.at[pl.ds(0, N_TILE - 1)], TAGS)
    entry = iota((N_TILE, HALF), 1)
    placing = jnp.concatenate(
        [
            jnp.where(tag_in[:, 0, N_TILE * s : N_TILE * s + 1] == entry, 1.0, 0.0)
            for s in range(2)
        ],
        axis=0,
    ).astype(BF16)
    active = dot_tn(placing, jnp.ones((HALF, HALF), BF16))
    key_row, query_row = iota((HALF, HALF), 0), iota((HALF, HALF), 1)
    seen = (key_row // FRAMES == query_row // FRAMES) & (key_row <= query_row)
    mask[...] = jnp.where(seen, active, 0.0)
    active_wide = jnp.concatenate([active] * 4, axis=1) > 0.5
    loads[6].wait()
    rest = jnp.concatenate(
        [jnp.where(active_wide, cot[:, j, :].astype(F32), 0.0) for j in range(2)], axis=0
    ).astype(BF16)
    context_back(TEMPORAL, rest)

    for j in range(2):
        own = slice(j * HALF, (j + 1) * HALF)
        wait(recv_sem, box_in.at[0, j, pl.ds(0, N_TILE - 1)], STATES + j)
        start_row = j * N_TILE * 8
        spread[start_row : start_row + N_TILE * 8] = box_in[0, j].astype(F32).reshape(N_TILE * 8, HALF)
        rows = jnp.concatenate(
            [
                jnp.concatenate(
                    [spread[pl.ds(start_row + 4 * s + k, N_TILE, stride=8), :] for k in range(4)], axis=1
                )
                for s in range(2)
            ],
            axis=0,
        ).astype(BF16)
        grid[own] = dot_tn(placing, rows)
        project(TEMPORAL, grid[own], own)
        key_t[TEMPORAL, :, own] = key_n[TEMPORAL, own].T
        attend(TEMPORAL, 0, N_GROUP, (j,))
        attend_back(TEMPORAL, 0, N_GROUP, (j,))
        grid_grad = input_back(grid[own], rest[own], normed_back(TEMPORAL, own)).astype(BF16)
        back = dot(placing, grid_grad)
        for s in range(2):
            for k in range(4):
                spread[pl.ds(start_row + 4 * s + k, N_TILE, stride=8), :] = back[
                    s * N_TILE : (s + 1) * N_TILE, k * HALF : (k + 1) * HALF
                ]
        box_out[1, j] = spread[start_row : start_row + N_TILE * 8].reshape(N_TILE, 8, HALF).astype(BF16)
        box_in[1, j, t] = box_out[1, j, t]
        send_all(lambda to: box_out.at[1, j, to], box_in.at[1, j], GRADS + j)

    context_sum(TEMPORAL, rest)
    normed_t[TEMPORAL] = normed_n[TEMPORAL].T
    for g in range(N_GROUP):
        normed_sum(TEMPORAL, g)
    temporal = grid[...] + dot_tn(context_t[TEMPORAL], weights[7])
    for j in range(2):
        mixed_out[:, j, :] = jnp.where(active_wide, temporal[j * HALF : (j + 1) * HALF], 0.0).astype(BF16)
    stores[0].start()
    for g in range(N_GROUP):
        sum_core(TEMPORAL, g)

    for j in range(2):
        wait(recv_sem, box_in.at[1, j, pl.ds(0, N_TILE - 1)], GRADS + j)
    spread[...] = jnp.concatenate(
        [box_in[1, j].astype(F32) for j in range(2)], axis=1
    ).reshape(N_TILE * 16, HALF)
    rest = jnp.concatenate(
        [
            jnp.concatenate([spread[pl.ds(4 * s + k, HALF, stride=8), :] for k in range(4)], axis=1)
            for s in range(2)
        ],
        axis=0,
    ).astype(BF16)
    context_sum(SPATIAL, rest)
    context_back(SPATIAL, rest)
    for g in range(N_GROUP):
        attend_back(SPATIAL, g, g + 1, both)
        normed_sum(SPATIAL, g)
        if g > 0:
            sum_core(SPATIAL, g - 1)
        if g == 1:
            for group in range(N_GROUP):
                sum_first(TEMPORAL, group)
    grad_normed = normed_back(SPATIAL, whole)
    sum_core(SPATIAL, N_GROUP - 1)
    grad_out[...] = input_back(blocks[...].astype(F32), rest, grad_normed).astype(BF16)
    stores[1].start()
    sum_first(SPATIAL, 0)
    sum_first(SPATIAL, 1)
    sum_second(TEMPORAL)
    sum_first(SPATIAL, 2)
    sum_first(SPATIAL, 3)
    sum_last(TEMPORAL)
    sum_second(SPATIAL)
    sum_last(SPATIAL)
    stores[2].start()

    wait(send_sem, tag_in.at[pl.ds(0, N_TILE - 1)], TAGS)
    for j in range(2):
        wait(send_sem, box_in.at[0, j, pl.ds(0, N_TILE - 1)], STATES + j)
        wait(send_sem, box_in.at[1, j, pl.ds(0, N_TILE - 1)], GRADS + j)
    for piece in range(2):
        for g in range(N_GROUP):
            wait(send_sem, got_core.at[piece, g], CORE + 4 * piece + g)
            wait(send_sem, got_one.at[piece, g], FIRST + 4 * piece + g)
            wait(send_sem, got_two.at[piece, g], SECOND + 4 * piece + g)
        wait(send_sem, got_last.at[piece], LAST + piece)
    for store in stores:
        store.wait()


def hand_over(*refs):
    sources, targets, held, sem_in, sem_out = refs[:3], refs[3:6], refs[6:9], refs[9], refs[10]
    loads = [pltpu.make_async_copy(sources[i], held[i], sem_in.at[i]) for i in range(3)]
    stores = [pltpu.make_async_copy(held[i], targets[i], sem_out.at[i]) for i in range(3)]
    for load in loads:
        load.start()
    for load, store in zip(loads, stores):
        load.wait()
        store.start()
    for store in stores:
        store.wait()


def body(blocks, block_position, block_frame, block_count, weights, cotangent):
    unit = (16, HALF)
    pair = (2, ROWS, WIDTH)
    turned = (2, WIDTH, ROWS)
    hbm = pl.BlockSpec(memory_space=pltpu.HBM)
    out_shape = (
        jax.ShapeDtypeStruct((HALF, 2, WIDTH), BF16),
        jax.ShapeDtypeStruct((ROWS, WIDTH), BF16),
        jax.ShapeDtypeStruct((2, 8, WIDTH), F32),
    )
    results = pl.pallas_call(
        kernel,
        out_shape=out_shape,
        in_specs=[hbm] * 6,
        out_specs=(hbm, hbm, hbm),
        scratch_shapes=[
            pltpu.VMEM((HALF, 2, WIDTH), BF16),
            pltpu.VMEM((ROWS, WIDTH), BF16),
            pltpu.VMEM((2, 8, WIDTH), F32),
            pltpu.VMEM((1, 2), jnp.int32),
            pltpu.VMEM((1, 2), jnp.int32),
            pltpu.VMEM((1, 1), jnp.int32),
            pltpu.VMEM((ROWS, WIDTH), BF16),
            pltpu.VMEM((8, WIDTH, WIDTH), BF16),
            pltpu.VMEM((8, WIDTH, WIDTH), BF16),
            pltpu.VMEM((HALF, 2, WIDTH), BF16),
            pltpu.VMEM((HALF, HALF), F32),
            pltpu.VMEM((1, HALF), jnp.int32),
            pltpu.VMEM((N_TILE, 1, HALF), jnp.int32),
            pltpu.VMEM((N_TILE * 16, HALF), F32),
            pltpu.VMEM((2, 2, N_TILE, 8, HALF), BF16),
            pltpu.VMEM((2, 2, N_TILE, 8, HALF), BF16),
            pltpu.VMEM(pair, BF16),
            pltpu.VMEM(turned, BF16),
            pltpu.VMEM(pair, BF16),
            pltpu.VMEM((WIDTH, ROWS), BF16),
            pltpu.VMEM(pair, BF16),
            pltpu.VMEM(turned, BF16),
            pltpu.VMEM(pair, BF16),
            pltpu.VMEM((WIDTH, ROWS), BF16),
            pltpu.VMEM(turned, BF16),
            pltpu.VMEM((2, N_GROUP, 2, HALF, GROUP * HALF), BF16),
            pltpu.VMEM((ROWS, WIDTH), BF16),
            pltpu.VMEM((WIDTH, ROWS), BF16),
            pltpu.VMEM((2, 3, ROWS, WIDTH), BF16),
            pltpu.VMEM((ROWS, WIDTH), F32),
            pltpu.VMEM((2, 2, N_GROUP, 4, N_Y, N_PAIR) + unit, BF16),
            pltpu.VMEM((2, N_GROUP, 4, N_Y, N_PAIR) + unit, BF16),
            pltpu.VMEM((2, N_GROUP, 4, 4, N_PAIR) + unit, BF16),
            pltpu.VMEM((2, N_GROUP, 3, 4, N_PAIR) + unit, BF16),
            pltpu.VMEM((2, N_GROUP, 4, N_PAIR) + unit, BF16),
            pltpu.VMEM((2, N_GROUP, 3, N_PAIR) + unit, BF16),
            pltpu.VMEM((2, N_Z, 2) + unit, BF16),
            pltpu.VMEM((2, N_Z - 1, 2) + unit, BF16),
            pltpu.SemaphoreType.DMA((7,)),
            pltpu.SemaphoreType.DMA((3,)),
            pltpu.SemaphoreType.DMA((N_SEM,)),
            pltpu.SemaphoreType.DMA((N_SEM,)),
        ],
        compiler_params=pltpu.CompilerParams(
            collective_id=0, has_side_effects=True, vmem_limit_bytes=62 * 1024 * 1024
        ),
    )(
        block_position,
        block_frame,
        block_count,
        blocks.reshape(ROWS, WIDTH),
        weights,
        cotangent.reshape(HALF, 2, WIDTH),
    )
    mixed, input_grad, weight_grad = pl.pallas_call(
        hand_over,
        out_shape=out_shape,
        in_specs=[hbm] * 3,
        out_specs=(hbm, hbm, hbm),
        scratch_shapes=[pltpu.VMEM(leaf.shape, leaf.dtype) for leaf in out_shape]
        + [pltpu.SemaphoreType.DMA((3,))] * 2,
        compiler_params=pltpu.CompilerParams(vmem_limit_bytes=62 * 1024 * 1024),
        name="hand_over",
    )(*results)
    return mixed.reshape(cotangent.shape), input_grad.reshape(blocks.shape), weight_grad


def solution(mesh):
    return jax.shard_map(
        body,
        mesh=mesh,
        in_specs=(
            P("scene", "tile", None, None),
            P("scene", "tile"),
            P("scene", "tile"),
            P("scene", "tile"),
            P(),
            P("scene", None, None, "tile", None),
        ),
        out_specs=(
            P("scene", None, None, "tile", None),
            P("scene", "tile", None, None),
            P(None, ("scene", "tile"), None),
        ),
        check_vma=False,
    )
```

```python
import functools

import jax
import jax.numpy as jnp
from jax import lax
from jax.experimental import pallas as pl
from jax.experimental.pallas import tpu as pltpu
from jax.sharding import PartitionSpec as P

MESH = pl.DeviceIdType.MESH
N_X, N_Y, N_Z, N_TILE = 4, 4, 8, 64
HEADS, HEAD_DIM = 16, 32
WIDTH, ROWS, HALF = 512, 256, 128
FRAMES = 8
GROUP = 4
EPSILON = 1e-06
SPATIAL, TEMPORAL = 0, 1
BF16, F32 = jnp.bfloat16, jnp.float32
EXP2_SCALE = HEAD_DIM ** (-0.5) * 1.4426950408889634
SCALE = HEAD_DIM ** (-0.5)
TAGS, STATES, GRADS, CORE, FIRST, SECOND, LAST = 0, 1, 3, 5, 13, 21, 29
N_SEM = 31
N_GROUP = HEADS // GROUP
N_PAIR = N_Z // 2


def dot(left, right):
    return jnp.dot(left, right, preferred_element_type=F32)


def dot_tn(left, right):
    return lax.dot_general(left, right, (((0,), (0,)), ((), ())), preferred_element_type=F32)


def dot_nt(left, right):
    return lax.dot_general(left, right, (((1,), (1,)), ((), ())), preferred_element_type=F32)


def iota(shape, axis):
    return lax.broadcasted_iota(jnp.int32, shape, axis)


def tile_index(y, z, core):
    return (y * N_Z + z) * 2 + core


def inverse_norm(rows):
    return lax.rsqrt(jnp.mean(rows * rows, axis=-1, keepdims=True) + EPSILON)


def kernel(
    position_in,
    frame_in,
    count_in,
    blocks_in,
    weights_in,
    cot_in,
    mixed_to,
    grad_to,
    weight_to,
    mixed_out,
    grad_out,
    weight_out,
    position,
    frame,
    count,
    blocks,
    weights,
    weights_t,
    cot,
    mask,
    tag_out,
    tag_in,
    spread,
    box_out,
    box_in,
    normed_n,
    normed_t,
    query_n,
    query_t,
    key_n,
    key_t,
    value_n,
    value_t,
    context_t,
    soft_t,
    grad_context_n,
    grad_context_t,
    grad_n,
    grid,
    parts,
    got_core,
    sum_one,
    got_one,
    sum_two,
    got_two,
    last,
    got_last,
    in_sem,
    out_sem,
    send_sem,
    recv_sem,
):
    loads = [
        pltpu.make_async_copy(source, target, in_sem.at[i])
        for i, (source, target) in enumerate(
            [
                (blocks_in, blocks),
                (weights_in.at[pl.ds(0, 3)], weights.at[pl.ds(0, 3)]),
                (position_in, position),
                (frame_in, frame),
                (count_in, count),
                (weights_in.at[pl.ds(3, 5)], weights.at[pl.ds(3, 5)]),
                (cot_in, cot),
            ]
        )
    ]
    for load in loads:
        load.start()
    stores = [
        pltpu.make_async_copy(source, target, out_sem.at[i])
        for i, (source, target) in enumerate(
            [(mixed_out, mixed_to), (grad_out, grad_to), (weight_out, weight_to)]
        )
    ]

    x = lax.axis_index("scene")
    t = lax.axis_index("tile")
    core, z, y = lax.rem(t, 2), lax.rem(t // 2, N_Z), t // (2 * N_Z)
    peer_core = (x, tile_index(y, z, 1 - core))
    peers_x = [(lax.rem(x + d, N_X), t) for d in range(1, N_X)]
    peers_y = [(x, tile_index(lax.rem(y + d, N_Y), z, core)) for d in range(1, N_Y)]
    peers_z = [(x, tile_index(y, lax.rem(z + d, N_Z), core)) for d in range(1, N_Z)]

    barrier = pltpu.get_barrier_semaphore()

    for d in range(1, N_TILE):
        pl.semaphore_signal(
            barrier, inc=1, device_id=(x, lax.rem(t + d, N_TILE)), device_id_type=MESH
        )

    for peer in peers_x:
        pl.semaphore_signal(barrier, inc=1, device_id=peer, device_id_type=MESH)

    def start(source, target, sem, peer):
        pltpu.make_async_remote_copy(
            src_ref=source,
            dst_ref=target,
            send_sem=send_sem.at[sem],
            recv_sem=recv_sem.at[sem],
            device_id=peer,
            device_id_type=MESH,
        ).start()

    def wait(sems, ref, sem):
        pltpu.make_async_copy(ref, ref, sems.at[sem]).wait()

    def send_all(outgoing, incoming, sem):
        @pl.loop(1, N_TILE)
        def _(d):
            to = lax.rem(t + d, N_TILE)
            start(outgoing(to), incoming.at[t], sem, (x, to))

    def project(piece, rows, own):
        scaled = (rows * inverse_norm(rows)).astype(BF16)
        normed_n[piece, own] = scaled
        first = 4 * piece
        queries = dot(scaled, weights[first]).astype(BF16)
        query_n[piece, own] = queries
        query_t[:, own] = queries.T
        key_n[piece, own] = dot(scaled, weights[first + 1]).astype(BF16)
        values = dot(scaled, weights[first + 2]).astype(BF16)
        value_n[piece, own] = values
        value_t[:, own] = values.T

    def one_head(rows, h, axis):
        owner = iota((HALF, HALF), axis) // HEAD_DIM
        return jnp.where(owner == h, rows, jnp.zeros_like(rows))

    def by_head(rows, axis):
        return jnp.concatenate([one_head(rows, h, axis) for h in range(GROUP)], axis=1 - axis)

    def attend(piece, lower, upper, halves):
        for g in range(lower, upper):
            feats = slice(g * HALF, (g + 1) * HALF)
            for b in halves:
                own = slice(b * HALF, (b + 1) * HALF)
                queries = query_t[feats, own]
                keys = key_n[piece, own, feats]
                for h in range(GROUP):
                    scores = dot(keys, one_head(queries, h, 0))
                    if piece == TEMPORAL:
                        scores = jnp.where(mask[...] > 0.5, scores, -1e30)
                    top = jnp.max(scores, axis=0, keepdims=True)
                    powers = jnp.exp2((scores - top) * EXP2_SCALE)
                    share = 1.0 / jnp.sum(powers, axis=0, keepdims=True)
                    soft = (powers * share).astype(BF16)
                    soft_t[piece, g, b, :, h * HALF : (h + 1) * HALF] = soft
                    head = slice(g * HALF + h * HEAD_DIM, g * HALF + (h + 1) * HEAD_DIM)
                    context_t[piece, head, own] = dot(value_t[head, own], soft).astype(BF16)

    def attend_back(piece, lower, upper, halves):
        for g in range(lower, upper):
            feats = slice(g * HALF, (g + 1) * HALF)
            for b in halves:
                own = slice(b * HALF, (b + 1) * HALF)
                grads_t = grad_context_t[feats, own]
                values = value_n[piece, own, feats]
                soft = soft_t[piece, g, b]
                grad_scores, grad_queries = [], []
                for h in range(GROUP):
                    wide = soft[:, h * HALF : (h + 1) * HALF].astype(F32)
                    grad_soft = dot(values, one_head(grads_t, h, 0))
                    mean = jnp.sum(wide * grad_soft, axis=0, keepdims=True)
                    grad_scores.append((wide * (grad_soft - mean)).astype(BF16))
                    head = slice(g * HALF + h * HEAD_DIM, g * HALF + (h + 1) * HEAD_DIM)
                    grad_queries.append(dot(key_t[piece, head, own], grad_scores[h]))
                grad_queries = jnp.concatenate(grad_queries, axis=0)
                grad_n[piece, 0, own, feats] = (grad_queries * SCALE).T.astype(BF16)
                grad_keys = dot(
                    jnp.concatenate(grad_scores, axis=1), by_head(query_n[piece, own, feats], 1)
                )
                grad_n[piece, 1, own, feats] = (grad_keys * SCALE).astype(BF16)
                grad_values = dot(soft, by_head(grad_context_n[own, feats], 1))
                grad_n[piece, 2, own, feats] = grad_values.astype(BF16)

    def context_back(piece, rest):
        grads = dot(rest, weights_t[4 * piece + 3]).astype(BF16)
        grad_context_n[...] = grads
        grad_context_t[...] = grads.T

    def normed_back(piece, own):
        first = 4 * piece
        return (
            dot(grad_n[piece, 0, own], weights_t[first])
            + dot(grad_n[piece, 1, own], weights_t[first + 1])
            + dot(grad_n[piece, 2, own], weights_t[first + 2])
        )

    def input_back(rows, rest, grad_normed):
        inverse = inverse_norm(rows)
        scaled = rows * inverse
        along = jnp.mean(scaled * grad_normed, axis=-1, keepdims=True)
        return rest.astype(F32) + inverse * (grad_normed - scaled * along)

    def put_part(piece, g, w, product):
        split = product.reshape(N_Y * N_Z, 2, 8, HALF)
        for c in range(2):
            parts[piece, c, g, w] = (
                split[:, c].reshape(N_Y, N_PAIR, 16, HALF).astype(BF16)
            )

    def context_sum(piece, rest):
        product = dot(context_t[piece], rest)
        for g in range(N_GROUP):
            put_part(piece, g, 3, product[:, g * HALF : (g + 1) * HALF])

    def normed_sum(piece, g):
        chunk = slice(g * HALF, (g + 1) * HALF)
        grads = jnp.concatenate([grad_n[piece, w, :, chunk] for w in range(3)], axis=1)
        product = dot(normed_t[piece], grads)
        for w in range(3):
            put_part(piece, g, w, product[:, w * HALF : (w + 1) * HALF])
        start(parts.at[piece, 1 - core, g], got_core.at[piece, g], CORE + 4 * piece + g, peer_core)

    def add_up(own, got, n):
        total = own.astype(F32)
        for d in range(n - 1):
            total += got[d].astype(F32)
        return total

    def send_one(piece, g):
        me, peers = (x, peers_x) if g % 2 == 0 else (y, peers_y)
        for d in range(1, 4):
            start(sum_one.at[piece, g, lax.rem(me + d, 4)], got_one.at[piece, g, d - 1], FIRST + 4 * piece + g, peers[d - 1])

    def sum_core(piece, g):
        wait(recv_sem, got_core.at[piece, g], CORE + 4 * piece + g)
        for w in range(4):
            for j in range(N_Y):
                at = (w, j) if g % 2 == 0 else (j, w)
                sum_one[(piece, g) + at] = (
                    parts[piece, core, g, w, j].astype(F32) + got_core[piece, g, w, j].astype(F32)
                ).astype(BF16)
        send_one(piece, g)

    def sum_first(piece, g):
        first, second, peers = (x, y, peers_y) if g % 2 == 0 else (y, x, peers_x)
        wait(recv_sem, got_one.at[piece, g], FIRST + 4 * piece + g)
        sum_two[piece, g] = add_up(sum_one[piece, g, first], [got_one[piece, g, d] for d in range(3)], 4).astype(BF16)
        for d in range(1, 4):
            start(sum_two.at[piece, g, lax.rem(second + d, 4)], got_two.at[piece, g, d - 1], SECOND + 4 * piece + g, peers[d - 1])

    def sum_second(piece):
        for s in range(2):
            halves = []
            for g in (2 * s, 2 * s + 1):
                second = y if g % 2 == 0 else x
                wait(recv_sem, got_two.at[piece, g], SECOND + 4 * piece + g)
                total = add_up(sum_two[piece, g, second], [got_two[piece, g, d] for d in range(3)], 4)
                halves.append(total.reshape(N_Z, 8, HALF))
            last[piece, :, s] = jnp.concatenate(halves, axis=1).astype(BF16)
        for d in range(1, N_Z):
            start(last.at[piece, lax.rem(z + d, N_Z)], got_last.at[piece, d - 1], LAST + piece, peers_z[d - 1])

    def sum_last(piece):
        wait(recv_sem, got_last.at[piece], LAST + piece)
        scaling = (N_X * N_TILE * ROWS) ** (-0.5)
        total = add_up(last[piece, z], [got_last[piece, d] for d in range(N_Z - 1)], N_Z) * scaling
        for s in range(2):
            for half in range(2):
                column = (2 * s + half) * HALF
                weight_out[piece, :, column : column + HALF] = total[s, 8 * half : 8 * half + 8]

    loads[0].wait()
    loads[1].wait()
    whole, both = slice(0, ROWS), (0, 1)
    project(SPATIAL, blocks[...].astype(F32), whole)

    attend(SPATIAL, 0, 3, both)
    lane = iota((1, HALF), 1)
    for i in range(2, 5):
        loads[i].wait()
    usable = iota((1, 2), 1) < count[:, 0:1]
    tags = jnp.where(usable, position[...] * FRAMES + frame[...], -1)
    tag_out[...] = jnp.where(lane < N_TILE, tags[:, 0:1], tags[:, 1:2])
    tag_in[t] = tag_out[...]
    pl.semaphore_wait(barrier, N_TILE - 1 + N_X - 1)
    send_all(lambda to: tag_out, tag_in, TAGS)

    attend(SPATIAL, 3, 4, both)
    loads[5].wait()
    states = blocks[...].astype(F32) + dot_tn(context_t[SPATIAL], weights[3])
    for s in range(2):
        for k in range(4):
            spread[pl.ds(4 * s + k, HALF, stride=8), :] = states[
                s * HALF : (s + 1) * HALF, k * HALF : (k + 1) * HALF
            ]
    for j in range(2):
        box_out[0, j] = spread[...].reshape(N_TILE, 2, 8, HALF)[:, j].astype(BF16)
        box_in[0, j, t] = box_out[0, j, t]
        send_all(lambda to: box_out.at[0, j, to], box_in.at[0, j], STATES + j)

    for w in range(8):
        weights_t[w] = weights[w].T
    normed_t[SPATIAL] = normed_n[SPATIAL].T
    key_t[SPATIAL] = key_n[SPATIAL].T

    wait(recv_sem, tag_in.at[pl.ds(0, N_TILE - 1)], TAGS)
    entry = iota((N_TILE, HALF), 1)
    placing = jnp.concatenate(
        [
            jnp.where(tag_in[:, 0, N_TILE * s : N_TILE * s + 1] == entry, 1.0, 0.0)
            for s in range(2)
        ],
        axis=0,
    ).astype(BF16)
    active = dot_tn(placing, jnp.ones((HALF, HALF), BF16))
    key_row, query_row = iota((HALF, HALF), 0), iota((HALF, HALF), 1)
    seen = (key_row // FRAMES == query_row // FRAMES) & (key_row <= query_row)
    mask[...] = jnp.where(seen, active, 0.0)
    active_wide = jnp.concatenate([active] * 4, axis=1) > 0.5
    loads[6].wait()
    rest = jnp.concatenate(
        [jnp.where(active_wide, cot[:, j, :].astype(F32), 0.0) for j in range(2)], axis=0
    ).astype(BF16)
    context_back(TEMPORAL, rest)

    for j in range(2):
        own = slice(j * HALF, (j + 1) * HALF)
        wait(recv_sem, box_in.at[0, j, pl.ds(0, N_TILE - 1)], STATES + j)
        start_row = j * N_TILE * 8
        spread[start_row : start_row + N_TILE * 8] = box_in[0, j].astype(F32).reshape(N_TILE * 8, HALF)
        rows = jnp.concatenate(
            [
                jnp.concatenate(
                    [spread[pl.ds(start_row + 4 * s + k, N_TILE, stride=8), :] for k in range(4)], axis=1
                )
                for s in range(2)
            ],
            axis=0,
        ).astype(BF16)
        grid[own] = dot_tn(placing, rows)
        project(TEMPORAL, grid[own], own)
        key_t[TEMPORAL, :, own] = key_n[TEMPORAL, own].T
        attend(TEMPORAL, 0, N_GROUP, (j,))
        attend_back(TEMPORAL, 0, N_GROUP, (j,))
        grid_grad = input_back(grid[own], rest[own], normed_back(TEMPORAL, own)).astype(BF16)
        back = dot(placing, grid_grad)
        for s in range(2):
            for k in range(4):
                spread[pl.ds(start_row + 4 * s + k, N_TILE, stride=8), :] = back[
                    s * N_TILE : (s + 1) * N_TILE, k * HALF : (k + 1) * HALF
                ]
        box_out[1, j] = spread[start_row : start_row + N_TILE * 8].reshape(N_TILE, 8, HALF).astype(BF16)
        box_in[1, j, t] = box_out[1, j, t]
        send_all(lambda to: box_out.at[1, j, to], box_in.at[1, j], GRADS + j)

    context_sum(TEMPORAL, rest)
    normed_t[TEMPORAL] = normed_n[TEMPORAL].T
    for g in range(N_GROUP):
        normed_sum(TEMPORAL, g)
    temporal = grid[...] + dot_tn(context_t[TEMPORAL], weights[7])
    for j in range(2):
        mixed_out[:, j, :] = jnp.where(active_wide, temporal[j * HALF : (j + 1) * HALF], 0.0).astype(BF16)
    stores[0].start()
    for g in range(N_GROUP):
        sum_core(TEMPORAL, g)

    for j in range(2):
        wait(recv_sem, box_in.at[1, j, pl.ds(0, N_TILE - 1)], GRADS + j)
    spread[...] = jnp.concatenate(
        [box_in[1, j].astype(F32) for j in range(2)], axis=1
    ).reshape(N_TILE * 16, HALF)
    rest = jnp.concatenate(
        [
            jnp.concatenate([spread[pl.ds(4 * s + k, HALF, stride=8), :] for k in range(4)], axis=1)
            for s in range(2)
        ],
        axis=0,
    ).astype(BF16)
    context_sum(SPATIAL, rest)
    context_back(SPATIAL, rest)
    for g in range(N_GROUP):
        attend_back(SPATIAL, g, g + 1, both)
        if g > 0:
            sum_core(SPATIAL, g - 1)
        normed_sum(SPATIAL, g)
        if g == 2:
            for group in range(N_GROUP):
                sum_first(TEMPORAL, group)
    grad_normed = normed_back(SPATIAL, whole)
    sum_core(SPATIAL, N_GROUP - 1)
    grad_out[...] = input_back(blocks[...].astype(F32), rest, grad_normed).astype(BF16)
    stores[1].start()
    sum_first(SPATIAL, 0)
    sum_first(SPATIAL, 1)
    sum_second(TEMPORAL)
    sum_first(SPATIAL, 2)
    sum_first(SPATIAL, 3)
    sum_last(TEMPORAL)
    sum_second(SPATIAL)
    sum_last(SPATIAL)
    stores[2].start()

    wait(send_sem, tag_in.at[pl.ds(0, N_TILE - 1)], TAGS)
    for j in range(2):
        wait(send_sem, box_in.at[0, j, pl.ds(0, N_TILE - 1)], STATES + j)
        wait(send_sem, box_in.at[1, j, pl.ds(0, N_TILE - 1)], GRADS + j)
    for piece in range(2):
        for g in range(N_GROUP):
            wait(send_sem, got_core.at[piece, g], CORE + 4 * piece + g)
            wait(send_sem, got_one.at[piece, g], FIRST + 4 * piece + g)
            wait(send_sem, got_two.at[piece, g], SECOND + 4 * piece + g)
        wait(send_sem, got_last.at[piece], LAST + piece)
    for store in stores:
        store.wait()


def hand_over(*refs):
    sources, targets, held, sem_in, sem_out = refs[:3], refs[3:6], refs[6:9], refs[9], refs[10]
    pieces = [(i, pl.ds(q * n, n)) for i, n in ((0, HALF // 4), (1, ROWS // 4)) for q in range(4)] + [(2, pl.ds(0, 2))]
    loads = [pltpu.make_async_copy(sources[i].at[at], held[i].at[at], sem_in.at[q]) for q, (i, at) in enumerate(pieces)]
    stores = [pltpu.make_async_copy(held[i].at[at], targets[i].at[at], sem_out.at[q]) for q, (i, at) in enumerate(pieces)]
    for load in loads:
        load.start()
    for load, store in zip(loads, stores):
        load.wait()
        store.start()
    for store in stores:
        store.wait()


def body(blocks, block_position, block_frame, block_count, weights, cotangent):
    unit = (16, HALF)
    pair = (2, ROWS, WIDTH)
    turned = (2, WIDTH, ROWS)
    hbm = pl.BlockSpec(memory_space=pltpu.HBM)
    out_shape = (
        jax.ShapeDtypeStruct((HALF, 2, WIDTH), BF16),
        jax.ShapeDtypeStruct((ROWS, WIDTH), BF16),
        jax.ShapeDtypeStruct((2, 8, WIDTH), F32),
    )
    results = pl.pallas_call(
        kernel,
        out_shape=out_shape,
        in_specs=[hbm] * 6,
        out_specs=(hbm, hbm, hbm),
        scratch_shapes=[
            pltpu.VMEM((HALF, 2, WIDTH), BF16),
            pltpu.VMEM((ROWS, WIDTH), BF16),
            pltpu.VMEM((2, 8, WIDTH), F32),
            pltpu.VMEM((1, 2), jnp.int32),
            pltpu.VMEM((1, 2), jnp.int32),
            pltpu.VMEM((1, 1), jnp.int32),
            pltpu.VMEM((ROWS, WIDTH), BF16),
            pltpu.VMEM((8, WIDTH, WIDTH), BF16),
            pltpu.VMEM((8, WIDTH, WIDTH), BF16),
            pltpu.VMEM((HALF, 2, WIDTH), BF16),
            pltpu.VMEM((HALF, HALF), F32),
            pltpu.VMEM((1, HALF), jnp.int32),
            pltpu.VMEM((N_TILE, 1, HALF), jnp.int32),
            pltpu.VMEM((N_TILE * 16, HALF), F32),
            pltpu.VMEM((2, 2, N_TILE, 8, HALF), BF16),
            pltpu.VMEM((2, 2, N_TILE, 8, HALF), BF16),
            pltpu.VMEM(pair, BF16),
            pltpu.VMEM(turned, BF16),
            pltpu.VMEM(pair, BF16),
            pltpu.VMEM((WIDTH, ROWS), BF16),
            pltpu.VMEM(pair, BF16),
            pltpu.VMEM(turned, BF16),
            pltpu.VMEM(pair, BF16),
            pltpu.VMEM((WIDTH, ROWS), BF16),
            pltpu.VMEM(turned, BF16),
            pltpu.VMEM((2, N_GROUP, 2, HALF, GROUP * HALF), BF16),
            pltpu.VMEM((ROWS, WIDTH), BF16),
            pltpu.VMEM((WIDTH, ROWS), BF16),
            pltpu.VMEM((2, 3, ROWS, WIDTH), BF16),
            pltpu.VMEM((ROWS, WIDTH), F32),
            pltpu.VMEM((2, 2, N_GROUP, 4, N_Y, N_PAIR) + unit, BF16),
            pltpu.VMEM((2, N_GROUP, 4, N_Y, N_PAIR) + unit, BF16),
            pltpu.VMEM((2, N_GROUP, 4, 4, N_PAIR) + unit, BF16),
            pltpu.VMEM((2, N_GROUP, 3, 4, N_PAIR) + unit, BF16),
            pltpu.VMEM((2, N_GROUP, 4, N_PAIR) + unit, BF16),
            pltpu.VMEM((2, N_GROUP, 3, N_PAIR) + unit, BF16),
            pltpu.VMEM((2, N_Z, 2) + unit, BF16),
            pltpu.VMEM((2, N_Z - 1, 2) + unit, BF16),
            pltpu.SemaphoreType.DMA((7,)),
            pltpu.SemaphoreType.DMA((3,)),
            pltpu.SemaphoreType.DMA((N_SEM,)),
            pltpu.SemaphoreType.DMA((N_SEM,)),
        ],
        compiler_params=pltpu.CompilerParams(
            collective_id=0, has_side_effects=True, vmem_limit_bytes=62 * 1024 * 1024
        ),
    )(
        block_position,
        block_frame,
        block_count,
        blocks.reshape(ROWS, WIDTH),
        weights,
        cotangent.reshape(HALF, 2, WIDTH),
    )
    mixed, input_grad, weight_grad = pl.pallas_call(
        hand_over,
        out_shape=out_shape,
        in_specs=[hbm] * 3,
        out_specs=(hbm, hbm, hbm),
        scratch_shapes=[pltpu.VMEM(leaf.shape, leaf.dtype) for leaf in out_shape]
        + [pltpu.SemaphoreType.DMA((9,))] * 2,
        compiler_params=pltpu.CompilerParams(vmem_limit_bytes=62 * 1024 * 1024),
        name="hand_over",
    )(*results)
    return mixed.reshape(cotangent.shape), input_grad.reshape(blocks.shape), weight_grad


def solution(mesh):
    return jax.shard_map(
        body,
        mesh=mesh,
        in_specs=(
            P("scene", "tile", None, None),
            P("scene", "tile"),
            P("scene", "tile"),
            P("scene", "tile"),
            P(),
            P("scene", None, None, "tile", None),
        ),
        out_specs=(
            P("scene", None, None, "tile", None),
            P("scene", "tile", None, None),
            P(None, ("scene", "tile"), None),
        ),
        check_vma=False,
    )
```
